256 devices in a mesh: rad: 16 (over y, x_lo, core), azi: 16 (over x_hi, z).
Axes of the slice: x: 4 (x_hi: 2, x_lo: 2; x = x_hi * 2 + x_lo), y: 4, z: 8, core: 2. Of those that a mesh axis runs over, the one named last changes fastest.
Arguments:
- positions: float32 [3, 4194304], P(None, ('rad', 'azi')), may hold values from 0 to 1
- velocities: float32 [3, 4194304], P(None, ('rad', 'azi')), may hold values from -3 to 3
- masses: float32 [4194304], P(('rad', 'azi')), may hold values from 0.5 to 2
- neighbours: int32 [32768, 4], P(('rad', 'azi')), may hold values from 0 to 143, as said below
- shear_offsets: int32 [2, 16], replicated, may hold values from 0 to 15
- destinations: int32 [32768], P(('rad', 'azi')), may hold values from 0 to 15, as said below
- deposit_cells: int32 [2, 4194304], P(None, ('rad', 'azi')), may hold values from 0 to 4095
- old_potential: float32 [1024, 1024], P('rad', 'azi'), may hold values from -6 to 6
Outputs:
- migrated: float32 [7, 16777216], P(None, ('rad', 'azi'))
- potential: float32 [1024, 1024], P('rad', 'azi')
The draws below stay inside these ranges and needn't reach their ends.
Inputs may be any that keep to these rules, and one draw needn't show every extreme that they name: `neighbours`: entries index a device's table of 128 own tiles and 16 ghost tiles; the first entry of each tile's list is the tile itself, and each ghost tile is listed by some tile of every device. `destinations`: one device sends at most 32 tiles to any one azimuthal strip and a device receives at most 512 tiles; in every radial strip one azimuthal strip receives exactly 32 tiles from each device of that radial strip.
All inputs are finite; a program needn't handle non-finite values.
Results may differ from the reference program's by a relative error of at most 0.0003.
Values sent between devices are 32-bit elements; how exact they have to be, the bound alone decides.
No kernel may reach another device: no remote copies, remote signals or barrier semaphores. Data moves between devices by JAX's collectives and lax.ppermute only.
A program may use at most 64 MiB of HBM per device.

```python
import math
import jax
import jax.numpy as jnp
from jax import lax

TILES = 128
TILE = 128
EDGE = 4
LINKS = 4
GX = 64
GY = 64
STEPS = 2
SLOT = 32
CAP = 512
PART = 4194304
NX = 1024
NY = 1024
N_RAD = 16
N_AZI = 16


def draw_neighbours(key, part):
    devices = N_RAD * N_AZI
    lists_drawn = jax.random.randint(jax.random.fold_in(key, 11), (devices, TILES, LINKS), 0, TILES + 4 * EDGE)
    own_ids = jnp.arange(TILES, dtype=jnp.int32)
    lists_drawn = lists_drawn.at[:, :, 0].set(own_ids[None, :])
    scores = jax.random.randint(jax.random.fold_in(key, 12), (devices, TILES), 0, 1 << 20) * TILES + own_ids[None, :]
    ordering = jnp.argsort(scores, axis=1)
    chosen = ordering[:, :4 * EDGE]
    ghost_ids = TILES + jnp.arange(4 * EDGE, dtype=jnp.int32)
    device_ids = jnp.arange(devices, dtype=jnp.int32)
    lists_drawn = lists_drawn.at[device_ids[:, None], chosen, 1].set(ghost_ids[None, :])
    return lists_drawn.reshape(devices * TILES, LINKS).astype(jnp.int32)


def draw_destinations(key, part):
    slot_cap = TILES // 4
    hot_strip = jax.random.randint(jax.random.fold_in(key, 21), (N_RAD,), 0, N_AZI)
    rotation = jax.random.randint(jax.random.fold_in(key, 22), (N_RAD, N_AZI), 0, N_AZI - 1)
    tile_ids = jnp.arange(TILES, dtype=jnp.int32)
    scores = jax.random.randint(jax.random.fold_in(key, 23), (N_RAD, N_AZI, TILES), 0, 1 << 20) * TILES + tile_ids
    ranking = jnp.argsort(jnp.argsort(scores, axis=2), axis=2)
    spread = (hot_strip[:, None, None] + 1 + (ranking - slot_cap + rotation[:, :, None]) % (N_AZI - 1)) % N_AZI
    dest_strip = jnp.where(ranking < slot_cap, hot_strip[:, None, None], spread)
    return dest_strip.reshape(-1).astype(jnp.int32)


def plant(array, stream_key, least, largest):
    spot = [jax.random.randint(jax.random.fold_in(stream_key, axis), (), 0, length) for axis, length in enumerate(array.shape)]
    longest = array.shape.index(max(array.shape))
    neighbour = spot[:longest] + [(spot[longest] + 1) % array.shape[longest]] + spot[longest + 1:]
    return array.at[tuple(spot)].set(least).at[tuple(neighbour)].set(largest)


def block_levels(stream_key, extent, cuts, smallest, top_value):
    gain = 1.0
    for position, blocks in cuts:
        heights = jax.random.uniform(jax.random.fold_in(jax.random.fold_in(stream_key, 6), position), (blocks,), jnp.float32, smallest / len(cuts), top_value / len(cuts))
        gain = gain * jnp.repeat(jnp.exp(heights), extent[position] // blocks).reshape((-1,) + (1,) * (len(extent) - 1 - position))
    return gain


def gaussian(own_key, extent, scale, bound, shards=(), held_as=jnp.bfloat16):
    entries = jax.random.normal(own_key, extent, jnp.float32) * scale
    if len(shards) > 0:
        entries = block_levels(own_key, extent, shards, -0.22, 0.18) * entries
    return jnp.clip(entries, min=-bound, max=bound).astype(held_as)


def setup_inputs(seed: int = 0) -> dict:
    splits = jax.random.split(jax.random.key(seed), 9)
    return {
        "positions": jnp.clip(1.0 * jax.random.uniform(splits[0], (3, PART), jnp.float32) ** block_levels(splits[0], (3, PART), ((1, 256),), -0.2, 0.2), 0.0, 1.0),
        "velocities": gaussian(splits[1], (3, PART), 0.5, 3.0, ((1, 256),), jnp.float32),
        "masses": jnp.clip(jnp.exp(math.log(2.0) - 1.3862944 * jax.random.uniform(splits[2], (PART,), jnp.float32) ** block_levels(splits[2], (PART,), ((0, 256),), -0.2, 0.2)), 0.5, 2.0),
        "neighbours": draw_neighbours(jax.random.fold_in(splits[8], 71), 0),
        "shear_offsets": plant(jax.random.randint(splits[4], (STEPS, N_RAD), 0, N_AZI), jax.random.fold_in(splits[4], 1), 0, N_AZI - 1).astype(jnp.int32),
        "destinations": draw_destinations(jax.random.fold_in(splits[8], 71), 0),
        "deposit_cells": plant(jax.random.randint(splits[6], (STEPS, PART), 0, GX * GY), jax.random.fold_in(splits[6], 1), 0, (GX * GY) - 1).astype(jnp.int32),
        "old_potential": gaussian(splits[7], (NX, NY), 1.0, 6.0, ((0, 16), (1, 16)), jnp.float32),
    }


TIME_STEP = 0.1
ORBIT_FREQ = 0.3
CONTACT_STIFF = 0.15
INV_WIDTH = 4.0
GRAV_SCALE = 0.01


def contact_forces(own_tiles, table_all, neighbour_rows):
    groups = own_tiles.shape[1] // 4
    own_groups = jnp.transpose(own_tiles.reshape(4, groups, 4, -1), (1, 0, 2, 3))
    row_groups = neighbour_rows.reshape(groups, 4, -1)

    def one_group(group_args):
        own_part, row_part = group_args
        others = jnp.take(table_all, row_part, axis=1)
        offsets = own_part[:3, :, None, :, None] - others[:3, :, :, None, :]
        distance = jnp.sum(offsets * offsets, axis=0)
        weights = others[3][:, :, None, :] * jnp.exp(-INV_WIDTH * distance)
        return CONTACT_STIFF * jnp.sum(offsets * weights[None], axis=(2, 4))

    result = lax.map(one_group, (own_groups, row_groups))
    return jnp.transpose(result, (1, 0, 2, 3)).reshape(3, own_tiles.shape[1], -1)


def solve_potential(density):
    wave_x = jnp.arange(NX)
    wave_y = jnp.arange(NY)
    eigen_x = 4.0 * jnp.sin(jnp.pi * wave_x.astype(jnp.float32) / NX) ** 2
    eigen_y = 4.0 * jnp.sin(jnp.pi * wave_y.astype(jnp.float32) / NY) ** 2
    lam_grid = eigen_x[:, None] + eigen_y[None, :]
    at_zero = (wave_x[:, None] == 0) & (wave_y[None, :] == 0)
    green = jnp.where(at_zero, 0.0, -GRAV_SCALE / jnp.where(at_zero, 1.0, lam_grid))
    spectrum = jnp.fft.fft2(density) * green
    return jnp.real(jnp.fft.ifft2(spectrum)).astype(jnp.float32)


def per_device(device_args):
    own_tiles, table_all, neighbour_rows = device_args
    return contact_forces(own_tiles, table_all, neighbour_rows)


def reference(positions, velocities, masses, neighbours, shear_offsets, destinations, deposit_cells, old_potential):
    devices = N_RAD * N_AZI
    rad_ids = jnp.arange(N_RAD, dtype=jnp.int32)
    azi_ids = jnp.arange(N_AZI, dtype=jnp.int32)
    strip_x = (rad_ids - N_RAD // 2).astype(jnp.float32)
    place = positions.reshape(3, N_RAD, N_AZI, TILES, TILE)
    speed = velocities.reshape(3, N_RAD, N_AZI, TILES, TILE)
    mass_grid = masses.reshape(N_RAD, N_AZI, TILES, TILE)
    lists_all = neighbours.reshape(devices, TILES, LINKS)
    potential_now = old_potential
    for step_index in range(STEPS):
        cell_local = deposit_cells[step_index].reshape(N_RAD, N_AZI, TILES * TILE)
        cell_x = rad_ids[:, None, None] * GX + cell_local // GY
        cell_y = azi_ids[None, :, None] * GY + cell_local % GY
        grad_x = -(jnp.roll(potential_now, -1, 0) - jnp.roll(potential_now, 1, 0)) * 0.5
        grad_y = -(jnp.roll(potential_now, -1, 1) - jnp.roll(potential_now, 1, 1)) * 0.5
        gravity_x = grad_x[cell_x, cell_y].reshape(N_RAD, N_AZI, TILES, TILE)
        gravity_y = grad_y[cell_x, cell_y].reshape(N_RAD, N_AZI, TILES, TILE)
        density = jnp.zeros((NX, NY), jnp.float32).at[cell_x, cell_y].add(mass_grid.reshape(N_RAD, N_AZI, -1))
        next_potential = solve_potential(density)

        carried = jnp.concatenate([place, mass_grid[None]], axis=0)
        offsets_now = shear_offsets[step_index]
        below_rad = (rad_ids - 1) % N_RAD
        below_azi = (azi_ids[None, :] - offsets_now[:, None]) % N_AZI
        sheared_below = carried[:, below_rad[:, None], below_azi][:, :, :, EDGE:2 * EDGE]
        sheared_below = sheared_below.at[0].add(-1.0)
        above_rad = (rad_ids + 1) % N_RAD
        above_azi = (azi_ids[None, :] + offsets_now[above_rad][:, None]) % N_AZI
        sheared_above = carried[:, above_rad[:, None], above_azi][:, :, :, :EDGE]
        sheared_above = sheared_above.at[0].add(1.0)
        from_left = carried[:, :, (azi_ids - 1) % N_AZI][:, :, :, 3 * EDGE:4 * EDGE]
        from_left = from_left.at[1].add(-1.0)
        from_right = carried[:, :, (azi_ids + 1) % N_AZI][:, :, :, 2 * EDGE:3 * EDGE]
        from_right = from_right.at[1].add(1.0)
        table_all = jnp.concatenate([carried, sheared_below, sheared_above, from_left, from_right], axis=3)

        carried_dev = jnp.transpose(carried, (1, 2, 0, 3, 4)).reshape(devices, 4, TILES, TILE)
        table_dev = jnp.transpose(table_all, (1, 2, 0, 3, 4)).reshape(devices, 4, TILES + 4 * EDGE, TILE)
        forces = lax.map(per_device, (carried_dev, table_dev, lists_all))
        forces = jnp.transpose(forces.reshape(N_RAD, N_AZI, 3, TILES, TILE), (2, 0, 1, 3, 4))

        tidal_x = place[0] + strip_x[:, None, None, None]
        accel = jnp.stack([
            forces[0] + gravity_x + 2.0 * ORBIT_FREQ * speed[1] + 3.0 * ORBIT_FREQ ** 2 * tidal_x,
            forces[1] + gravity_y - 2.0 * ORBIT_FREQ * speed[0],
            forces[2] - ORBIT_FREQ ** 2 * (place[2] - 0.5)])
        speed = speed + TIME_STEP * accel
        place = place + TIME_STEP * speed
        potential_now = next_potential

    final_state = jnp.concatenate([place, speed, mass_grid[None]], axis=0)
    dest_strip = destinations.reshape(N_RAD, N_AZI, TILES)
    hit_table = (dest_strip[..., None] == azi_ids).astype(jnp.int32)
    earlier = jnp.cumsum(hit_table, axis=2) - hit_table
    rank_slot = jnp.sum(earlier * hit_table, axis=3)
    signed = ((azi_ids[None, :, None] - dest_strip + N_AZI // 2) % N_AZI) - N_AZI // 2
    final_state = final_state.at[1].add(signed.astype(jnp.float32)[..., None])
    target = (rad_ids[:, None, None] * N_AZI + dest_strip) * CAP + azi_ids[None, :, None] * SLOT + rank_slot
    migrated = jnp.zeros((7, devices * CAP, TILE), jnp.float32)
    migrated = migrated.at[:, target.reshape(-1)].set(final_state.reshape(7, -1, TILE))
    return migrated.reshape(7, -1), potential_now
```

```python
import functools
import math

import jax
import jax.numpy as jnp
import ml_dtypes
import numpy as np
from jax import lax
from jax.experimental import pallas as pl
from jax.experimental.pallas import tpu as pltpu
from jax.sharding import PartitionSpec as P

T = 128
TILES = 128
EDGE = 4
LINKS = 4
GHOSTS = 16
G = 64
SLOT = 32
STEPS = 2
DT = 0.1
OMEGA = 0.3
STIFF = 0.15
GRAV = 0.01
CEXP = 4.0 * math.log2(math.e)
CHUNK = 1024
F32 = jnp.float32
BF16 = jnp.bfloat16
VMEM = pl.BlockSpec(memory_space=pltpu.VMEM)
SMEM = pl.BlockSpec(memory_space=pltpu.SMEM)
EW = EDGE * T
NN = (((1,), (0,)), ((), ()))
NT = (((1,), (1,)), ((), ()))
TN = (((0,), (0,)), ((), ()))


def params():
    return pltpu.CompilerParams(vmem_limit_bytes=48 * 1024 * 1024)


def cost(us):
    return pl.CostEstimate(flops=int(us * 1.0e9), bytes_accessed=int(us * 3.0e6), transcendentals=0)


def dot(a, b, dims=NN):
    return lax.dot_general(a, b, dims, preferred_element_type=F32)


def split2(a):
    high = a.astype(BF16)
    return high, (a - high.astype(F32)).astype(BF16)


def split3(a):
    high = a.astype(BF16).astype(F32)
    rest = a - high
    mid = rest.astype(BF16).astype(F32)
    return high, mid, rest - mid


@functools.lru_cache(maxsize=None)
def tables(length, count):
    ids = np.arange(length, dtype=np.int64)
    angle = (ids[:, None] * ids[None, :] % length).astype(np.float64) * (2.0 * np.pi / length)
    full = (np.cos(angle) + np.sin(angle)) / math.sqrt(length)
    high = full.astype(ml_dtypes.bfloat16)
    low = (full - high.astype(np.float64)).astype(ml_dtypes.bfloat16)
    block = length // count
    rows = (np.arange(count)[:, None] * block - 1 + np.arange(block + 16)[None, :]) % length
    lam = (4.0 * np.sin(np.pi * ids / length) ** 2).astype(np.float32)
    return high, low, high[rows], low[rows], lam


def edges_kernel(pos_ref, mass_ref, pot_ref, up_ref, down_ref, right_ref, left_ref):
    pot = pot_ref[...]
    turned = pot.T
    halo = {
        1: pot[G - 1 : G, :],
        0: pot[0:1, :],
        3: turned[G - 1 : G, :],
        2: turned[0:1, :],
    }
    for ref, part in ((up_ref, 1), (down_ref, 0), (right_ref, 3), (left_ref, 2)):
        lanes = pl.ds(part * EW, EW)
        ref[0:3, 0:EW] = pos_ref[0:3, lanes]
        ref[3:4, 0:EW] = mass_ref[0:1, lanes]
        ref[:, EW : EW + 128] = jnp.zeros((4, 128), F32)
        ref[0:1, EW : EW + G] = halo[part]


def edges(pos, mass, pot):
    shape = jax.ShapeDtypeStruct((4, EW + 128), F32)
    return pl.pallas_call(
        edges_kernel,
        grid=(1,),
        in_specs=[
            pl.BlockSpec((3, 4 * EW), lambda i: (0, 0)),
            pl.BlockSpec((1, 4 * EW), lambda i: (0, 0)),
            pl.BlockSpec((G, G), lambda i: (0, 0)),
        ],
        out_specs=[pl.BlockSpec((4, EW + 128), lambda i: (0, 0))] * 4,
        out_shape=[shape] * 4,
        compiler_params=params(),
        cost_estimate=cost(1),
        name="edges",
    )(pos, mass, pot)


def density_kernel(cells_ref, mass_ref, dest_ref, dens_ref, target_ref, count_ref, acc_ref):
    lanes = cells_ref.shape[1]
    row = lax.broadcasted_iota(jnp.int32, (G, CHUNK), 0)
    acc_ref[...] = jnp.zeros_like(acc_ref)

    def body(j, carry):
        part = pl.ds(pl.multiple_of(j * CHUNK, CHUNK), CHUNK)
        mass = mass_ref[0:1, part]
        pieces = split3(mass)
        for s in range(STEPS):
            cell = cells_ref[s : s + 1, part]
            hit_x = row == (cell >> 6)
            hit_y = jnp.where(row == (cell & (G - 1)), 1.0, 0.0).astype(BF16)
            left = jnp.concatenate(
                [jnp.where(hit_x, piece, 0.0).astype(BF16) for piece in pieces], axis=0
            )
            acc_ref[s] += dot(left, hit_y, NT)
        return carry

    lax.fori_loop(0, lanes // CHUNK, body, 0)
    both = []
    for s in range(STEPS):
        both.append(acc_ref[s, 0:G] + acc_ref[s, G : 2 * G] + acc_ref[s, 2 * G : 3 * G])
    whole = jnp.concatenate(both, axis=1)
    for d in range(dens_ref.shape[0]):
        dens_ref[d] = whole

    for d in range(count_ref.shape[0]):
        count_ref[d] = 0

    def slot(t, carry):
        d = dest_ref[t]
        k = count_ref[d]
        target_ref[t] = d * SLOT + k
        count_ref[d] = k + 1
        return carry

    lax.fori_loop(0, TILES, slot, 0)


def densities(cells, mass, dest, copies, azi_count):
    return pl.pallas_call(
        density_kernel,
        in_specs=[VMEM, VMEM, SMEM],
        out_specs=[VMEM, SMEM],
        out_shape=[
            jax.ShapeDtypeStruct((copies, G, 2 * G), F32),
            jax.ShapeDtypeStruct((TILES,), jnp.int32),
        ],
        scratch_shapes=[
            pltpu.SMEM((azi_count,), jnp.int32),
            pltpu.VMEM((STEPS, 3 * G, G), F32),
        ],
        compiler_params=params(),
        cost_estimate=cost(7),
        name="densities",
    )(cells, mass, dest)


def dot3(a_high, a_low, b, dims=NN):
    b_high, b_low = split2(b)
    return dot(a_high, b_high, dims) + dot(a_high, b_low, dims) + dot(a_low, b_high, dims)


def forward_x_kernel(place_ref, high_ref, low_ref, dens_ref, out_ref):
    values = dens_ref[...].reshape(-1, 2 * G)
    lines = dot3(high_ref[0, 1 : G + 1], low_ref[0, 1 : G + 1], values)
    turned = lines.T
    whole = jnp.concatenate([turned[0:G], turned[G : 2 * G]], axis=1)
    for d in range(out_ref.shape[0]):
        out_ref[d] = whole


def solve_y_kernel(place_ref, high_ref, low_ref, some_high_ref, some_low_ref, lam_y_ref, lam_x_ref, in_ref, out_ref):
    values = in_ref[...].reshape(-1, 2 * G)
    lam_x = lam_x_ref[0, 0:1, :]
    mean = jnp.sum(values, axis=0, keepdims=True) * (1.0 / values.shape[0])
    values = values - jnp.where(lam_x == 0.0, mean, 0.0)
    modes = dot3(high_ref[...], low_ref[...], values)
    lam = lam_y_ref[...] + lam_x
    at_zero = lam == 0.0
    modes = modes * jnp.where(at_zero, 0.0, -GRAV / jnp.where(at_zero, 1.0, lam))
    lines = dot3(some_high_ref[0], some_low_ref[0], modes)
    inner = lines[1 : G + 1].T
    first = jnp.concatenate([inner[0:G], inner[G : 2 * G]], axis=1)
    for d in range(out_ref.shape[0]):
        out_ref[d, 0:G] = first
        out_ref[d, G : G + 8] = jnp.zeros((8, 2 * G), F32)
        out_ref[d, G : G + 1] = lines[0:1]
        out_ref[d, G + 1 : G + 2] = lines[G + 1 : G + 2]


def inverse_x_kernel(place_ref, high_ref, low_ref, in_ref, grad_ref, pot_ref, all_ref, halo_ref, turn_ref):
    count = in_ref.shape[0]
    halo_ref[...] = jnp.zeros_like(halo_ref)
    for d in range(count):
        all_ref[d * G : (d + 1) * G] = in_ref[d, 0:G]
        halo_ref[:, d * G : (d + 1) * G] = in_ref[d, G : G + 8, 0:G]
    grid = dot3(high_ref[0], low_ref[0], all_ref[...])
    pot_ref[...] = grid[1 : G + 1, G : 2 * G]
    b_high, b_low = split2(halo_ref[...])
    a_high, a_low = high_ref[0, 1 : G + 1], low_ref[0, 1 : G + 1]
    sides = dot(b_high, a_high, NT) + dot(b_low, a_high, NT) + dot(b_high, a_low, NT)
    grad_x = -(grid[2 : G + 2, 0:G] - grid[0:G, 0:G]) * 0.5
    turn_ref[8 : G + 8] = grid[1 : G + 1, 0:G].T
    turn_ref[7:8] = sides[0:1]
    turn_ref[G + 8 : G + 9] = sides[1:2]
    grad_y = (-(turn_ref[9 : G + 9] - turn_ref[7 : G + 7]) * 0.5).T
    write_gradient(grad_ref, grad_x, grad_y)


def write_gradient(grad_ref, grad_x, grad_y):
    for c, part in enumerate((grad_x, grad_y)):
        for p, piece in enumerate(split3(part)):
            grad_ref[c * G : (c + 1) * G, p * G : (p + 1) * G] = piece


def placed_block(shape):
    return pl.BlockSpec((1,) + shape, lambda i, place: (place[0],) + (0,) * len(shape))


def whole_block(shape):
    return pl.BlockSpec(shape, lambda i, place: (0,) * len(shape))


def placed_call(kernel, name, place, ins, outs, scratch=(), us=3):
    in_specs = [placed_block(a.shape[1:]) if by else whole_block(a.shape) for a, by in ins]
    return pl.pallas_call(
        kernel,
        grid_spec=pltpu.PrefetchScalarGridSpec(
            num_scalar_prefetch=1,
            grid=(1,),
            in_specs=in_specs,
            out_specs=[whole_block(o.shape) for o in outs],
            scratch_shapes=list(scratch),
        ),
        out_shape=list(outs),
        compiler_params=params(),
        cost_estimate=cost(us),
        name=name,
    )(place, *[a for a, _ in ins])


def exchange(value, axis):
    return lax.all_to_all(value, axis, split_axis=0, concat_axis=0, tiled=True)


def old_gradient(pot_ref, up_ref, down_ref, right_ref, left_ref, grad_ref, turn_ref):
    pot = pot_ref[...]
    turn_ref[8 : G + 8] = pot
    turn_ref[7:8] = up_ref[0:1, EW : EW + G]
    turn_ref[G + 8 : G + 9] = down_ref[0:1, EW : EW + G]
    grad_x = -(turn_ref[9 : G + 9] - turn_ref[7 : G + 7]) * 0.5
    turn_ref[8 : G + 8] = pot.T
    turn_ref[7:8] = right_ref[0:1, EW : EW + G]
    turn_ref[G + 8 : G + 9] = left_ref[0:1, EW : EW + G]
    grad_y = (-(turn_ref[9 : G + 9] - turn_ref[7 : G + 7]) * 0.5).T
    write_gradient(grad_ref, grad_x, grad_y)


def features(pos, mass, work_ref, i_ref, j_ref, r_ref, lanes, own):
    width = pos.shape[1]
    q = pos - 0.5
    norm = -CEXP * jnp.sum(q * q, axis=0, keepdims=True)
    one = jnp.ones_like(norm)
    n_high, n_mid, n_low = split3(norm)
    q_high, q_mid, q_low = split3(q)
    zero = jnp.zeros((8, width), F32)

    def write(groups, target_ref):
        for k, (three, last) in enumerate(groups):
            work_ref[4 * k : 4 * k + 3, 0:width] = three
            work_ref[4 * k + 3 : 4 * k + 4, 0:width] = last
        work_ref[24:32, 0:width] = zero
        target_ref[:, lanes] = work_ref[0:32, 0:width].astype(BF16)

    write(
        (
            (q_high, one),
            (q_mid, n_mid),
            (q_high, one),
            (q_low, n_low),
            (q_high, one),
            (q_mid, n_high),
        ),
        j_ref,
    )
    if own:
        a_high, a_mid, a_low = split3(q * (2.0 * CEXP))
        write(
            (
                (a_high, n_high),
                (a_high, one),
                (a_mid, n_mid),
                (a_high, one),
                (a_low, n_low),
                (a_mid, one),
            ),
            i_ref,
        )
    weighted = q * mass
    w_high = weighted.astype(BF16).astype(F32)
    m_high = mass.astype(BF16).astype(F32)
    work_ref[0:3, 0:width] = w_high
    work_ref[3:4, 0:width] = m_high
    work_ref[4:7, 0:width] = weighted - w_high
    work_ref[7:8, 0:width] = mass - m_high
    work_ref[8:16, 0:width] = zero
    r_ref[:, lanes] = work_ref[0:16, 0:width].astype(BF16)


def step_kernel(last, *refs):
    if last:
        (ints_ref, nbr_ref, target_ref, pos_ref, vel_ref, mass_ref, cells_ref, far_ref, right_ref, left_ref,
         grad_in_ref, pack_ref, i_ref, j_ref, r_ref, work_ref, grad_ref) = refs
    else:
        (ints_ref, nbr_ref, target_ref, pos_ref, vel_ref, mass_ref, cells_ref, far_ref, right_ref, left_ref,
         up_ref, down_ref, pot_ref, new_pos_ref, new_vel_ref, up_out, down_out, right_out, left_out, pack_ref,
         i_ref, j_ref, r_ref, work_ref, grad_ref, turn_ref, split_ref) = refs
    if last:
        grad_ref[...] = grad_in_ref[...].astype(BF16)
    else:
        old_gradient(pot_ref, up_ref, down_ref, right_ref, left_ref, split_ref, turn_ref)
        grad_ref[...] = split_ref[...].astype(BF16)
    pack_ref[...] = jnp.zeros_like(pack_ref)
    own_lanes = TILES * T

    def prepare(j, carry):
        lanes = pl.ds(pl.multiple_of(j * CHUNK, CHUNK), CHUNK)
        features(pos_ref[0:3, lanes], mass_ref[0:1, lanes], work_ref, i_ref, j_ref, r_ref, lanes, True)
        return carry

    lax.fori_loop(0, own_lanes // CHUNK, prepare, 0)

    below = far_ref[ints_ref[0], 0:4, :]
    above = far_ref[ints_ref[1], 4:8, :]
    sub = lax.broadcasted_iota(jnp.int32, (3, EW), 0)
    for e, (ghost, axis, move) in enumerate(
        ((below, 0, -1.0), (above, 0, 1.0), (right_ref[0:4, 0:EW], 1, -1.0), (left_ref[0:4, 0:EW], 1, 1.0))
    ):
        place = ghost[0:3] + jnp.where(sub == axis, move, 0.0)
        lanes = slice(own_lanes + e * EW, own_lanes + (e + 1) * EW)
        features(place, ghost[3:4], work_ref, i_ref, j_ref, r_ref, lanes, False)

    strip_x = ints_ref[2].astype(F32)
    row = lax.broadcasted_iota(jnp.int32, (G, T), 0)

    def tile(t, carry):
        own = pl.ds(pl.multiple_of(t * T, T), T)
        picks = [pl.ds(pl.multiple_of(nbr_ref[t, n] * T, T), T) for n in range(LINKS)]
        others = jnp.concatenate([j_ref[:, p] for p in picks], axis=1)
        right = jnp.concatenate([r_ref[:, p] for p in picks], axis=1)
        weights = jnp.exp2(dot(i_ref[:, own], others, TN)).astype(BF16)
        sums = dot(right, weights, NT)
        pos = pos_ref[0:3, own]
        vel = vel_ref[0:3, own]
        total = sums[0:4] + sums[4:8]
        contact = STIFF * ((pos - 0.5) * total[3:4] - total[0:3])
        cell = cells_ref[last : last + 1, own]
        hit_y = jnp.where(row == (cell & (G - 1)), 1.0, 0.0).astype(BF16)
        hit_x = row == (cell >> 6)
        field = dot(grad_ref[...], jnp.concatenate([hit_y] * 3, axis=0))
        grav_x = jnp.sum(jnp.where(hit_x, field[0:G], 0.0), axis=0, keepdims=True)
        grav_y = jnp.sum(jnp.where(hit_x, field[G : 2 * G], 0.0), axis=0, keepdims=True)
        acc_x = contact[0:1] + grav_x + 2.0 * OMEGA * vel[1:2] + 3.0 * OMEGA**2 * (pos[0:1] + strip_x)
        acc_y = contact[1:2] + grav_y - 2.0 * OMEGA * vel[0:1]
        acc_z = contact[2:3] - OMEGA**2 * (pos[2:3] - 0.5)
        speed = vel + DT * jnp.concatenate([acc_x, acc_y, acc_z], axis=0)
        target = target_ref[t]
        d = target // SLOT
        k = target % SLOT
        if last:
            for c in range(3):
                pack_ref[d, pl.ds(k * 3 + c, 1), :] = speed[c : c + 1]
        else:
            place = pos + DT * speed
            new_pos_ref[0:3, own] = place
            new_vel_ref[0:3, own] = speed
            pack_ref[d, k, 0:3, :] = place
            pack_ref[d, k, 3:4, :] = mass_ref[0:1, own]
        return carry

    lax.fori_loop(0, TILES, tile, 0, unroll=4)
    if not last:
        for ref, part in ((up_out, 1), (down_out, 0), (right_out, 3), (left_out, 2)):
            lanes = slice(part * EW, (part + 1) * EW)
            ref[0:3, :] = new_pos_ref[0:3, lanes]
            ref[3:4, :] = mass_ref[0:1, lanes]


def step(last, ints, nbr, target, pos, vel, mass, cells, far, right, left, more, azi_count):
    lanes = TILES * T
    if last:
        outs = [jax.ShapeDtypeStruct((azi_count, SLOT * 3, T), F32)]
        out_specs = [VMEM]
    else:
        outs = [jax.ShapeDtypeStruct((3, lanes), F32)] * 2 + [jax.ShapeDtypeStruct((4, EW), F32)] * 4
        outs += [jax.ShapeDtypeStruct((azi_count, SLOT, 4, T), F32)]
        out_specs = [VMEM] * 7
    scratch = [
        pltpu.VMEM((32, lanes), BF16),
        pltpu.VMEM((32, lanes + GHOSTS * T), BF16),
        pltpu.VMEM((16, lanes + GHOSTS * T), BF16),
        pltpu.VMEM((32, CHUNK), F32),
        pltpu.VMEM((2 * G, 3 * G), BF16),
    ]
    if not last:
        scratch += [pltpu.VMEM((G + 16, G), F32), pltpu.VMEM((2 * G, 3 * G), F32)]
    return pl.pallas_call(
        functools.partial(step_kernel, last),
        in_specs=[SMEM] * 3 + [VMEM] * (7 + len(more)),
        out_specs=out_specs,
        out_shape=outs,
        scratch_shapes=scratch,
        compiler_params=params(),
        cost_estimate=cost(20),
        name=f"step_{last}",
    )(ints, nbr, target, pos, vel, mass, cells, far, right, left, *more)


def assemble_kernel(azi_count, ints_ref, place_ref, speed_ref, out_ref):
    b = ints_ref[3]

    def group(g, carry):
        a = g // (SLOT // 8)
        h = g % (SLOT // 8)
        signed = lax.rem(a - b + azi_count // 2 + azi_count, azi_count) - azi_count // 2
        move = signed.astype(F32)
        speeds = speed_ref[a, pl.ds(pl.multiple_of(h * 24, 8), 24), :]
        sub = lax.broadcasted_iota(jnp.int32, (3, T), 0)
        for k in range(8):
            four = place_ref[a, h * 8 + k]
            speed = speeds[3 * k : 3 * k + 3]
            mass = four[3:4]
            place = four[0:3] + DT * speed
            place = place + jnp.where((sub == 1) & (mass > 0.0), move, 0.0)
            lanes = pl.ds(pl.multiple_of((g * 8 + k) * T, T), T)
            out_ref[0:3, lanes] = place
            out_ref[3:6, lanes] = speed
            out_ref[6:7, lanes] = mass
        return carry

    lax.fori_loop(0, azi_count * SLOT // 8, group, 0)


def assemble(ints, place, speed):
    azi_count = place.shape[0]
    return pl.pallas_call(
        functools.partial(assemble_kernel, azi_count),
        in_specs=[SMEM, VMEM, VMEM],
        out_specs=VMEM,
        out_shape=jax.ShapeDtypeStruct((7, azi_count * SLOT * T), F32),
        compiler_params=params(),
        cost_estimate=cost(4),
        name="assemble",
    )(ints, place, speed)


def shifted(value, axis, steps):
    count = lax.axis_size(axis)
    return lax.ppermute(value, axis, [(i, (i + steps) % count) for i in range(count)])


def local(positions, velocities, masses, neighbours, shear_offsets, destinations, deposit_cells, old_potential):
    rad_count = lax.axis_size("rad")
    azi_count = lax.axis_size("azi")
    r = lax.axis_index("rad")
    a = lax.axis_index("azi")
    mass = masses.reshape(1, -1)
    r_place = r.reshape(1).astype(jnp.int32)
    a_place = a.reshape(1).astype(jnp.int32)

    def ints(s):
        below = (a - shear_offsets[s, r]) % azi_count
        above = (a + shear_offsets[s, (r + 1) % rad_count]) % azi_count
        return jnp.stack([below, above, r - rad_count // 2, a]).astype(jnp.int32)

    def ghosts(up, down, right, left):
        up = shifted(up, "rad", 1)
        down = shifted(down, "rad", -1)
        right = shifted(right, "azi", 1)
        left = shifted(left, "azi", -1)
        both = jnp.concatenate([up[:, :EW], down[:, :EW]], axis=0)
        far = exchange(jnp.broadcast_to(both[None], (azi_count,) + both.shape), "azi")
        return far, up, down, right, left

    first, second = ints(0), ints(1)
    up, down, right, left = edges(positions, mass, old_potential)
    far, up, down, right, left = ghosts(up, down, right, left)

    dens, target = densities(deposit_cells, mass, destinations, rad_count, azi_count)
    high_x, low_x, rows_high_x, rows_low_x, lam_x = tables(G * rad_count, rad_count)
    high_y, low_y, rows_high_y, rows_low_y, lam_y = tables(G * azi_count, azi_count)
    lam_cols = np.tile(lam_x.reshape(rad_count, 1, G), (1, 8, 2))
    lam_rows = np.ascontiguousarray(np.broadcast_to(lam_y[:, None], (G * azi_count, 2 * G)))
    dens = exchange(dens, "rad")
    (lines,) = placed_call(
        forward_x_kernel, "forward_x", r_place,
        ((jnp.asarray(rows_high_x), True), (jnp.asarray(rows_low_x), True), (dens, False)),
        (jax.ShapeDtypeStruct((azi_count, G, 2 * G), F32),),
    )
    lines = exchange(lines, "azi")
    at = jnp.stack([r, a]).astype(jnp.int32)
    some = lambda table: pl.BlockSpec((1,) + table.shape[1:], lambda i, place: (place[1], 0, 0))
    (solved,) = pl.pallas_call(
        solve_y_kernel,
        grid_spec=pltpu.PrefetchScalarGridSpec(
            num_scalar_prefetch=1,
            grid=(1,),
            in_specs=[
                whole_block(high_y.shape), whole_block(low_y.shape), some(rows_high_y), some(rows_low_y),
                whole_block(lam_rows.shape), placed_block(lam_cols.shape[1:]), whole_block(lines.shape),
            ],
            out_specs=[whole_block((rad_count, G + 8, 2 * G))],
        ),
        out_shape=[jax.ShapeDtypeStruct((rad_count, G + 8, 2 * G), F32)],
        compiler_params=params(),
        cost_estimate=cost(6),
        name="solve_y",
    )(at, high_y, low_y, rows_high_y, rows_low_y, lam_rows, lam_cols, lines)
    solved = exchange(solved, "rad")
    gradient, potential = placed_call(
        inverse_x_kernel, "inverse_x", r_place,
        ((jnp.asarray(rows_high_x), True), (jnp.asarray(rows_low_x), True), (solved, False)),
        (jax.ShapeDtypeStruct((2 * G, 3 * G), F32), jax.ShapeDtypeStruct((G, G), F32)),
        (pltpu.VMEM((G * rad_count, 2 * G), F32), pltpu.VMEM((8, G * rad_count), F32), pltpu.VMEM((G + 16, G), F32)),
    )

    place, speed, up_1, down_1, right_1, left_1, pack_place = step(
        0, first, neighbours, target, positions, velocities, mass, deposit_cells, far, right, left,
        (up, down, old_potential), azi_count,
    )
    far_1, _, _, right_1, left_1 = ghosts(up_1, down_1, right_1, left_1)
    pack_place = exchange(pack_place, "azi")
    (pack_speed,) = step(
        1, second, neighbours, target, place, speed, mass, deposit_cells, far_1, right_1, left_1,
        (gradient,), azi_count,
    )
    pack_speed = exchange(pack_speed, "azi")
    return assemble(second, pack_place, pack_speed), potential


def solution(mesh):
    placed = (
        P(None, ("rad", "azi")),
        P(None, ("rad", "azi")),
        P(("rad", "azi")),
        P(("rad", "azi"), None),
        P(),
        P(("rad", "azi")),
        P(None, ("rad", "azi")),
        P("rad", "azi"),
    )
    return jax.shard_map(
        local,
        mesh=mesh,
        in_specs=placed,
        out_specs=(P(None, ("rad", "azi")), P("rad", "azi")),
        check_vma=False,
    )
```

```python
import functools
import math

import jax
import jax.numpy as jnp
import ml_dtypes
import numpy as np
from jax import lax
from jax.experimental import pallas as pl
from jax.experimental.pallas import tpu as pltpu
from jax.sharding import PartitionSpec as P

T = 128
TILES = 128
EDGE = 4
LINKS = 4
GHOSTS = 16
G = 64
SLOT = 32
STEPS = 2
DT = 0.1
OMEGA = 0.3
STIFF = 0.15
GRAV = 0.01
CEXP = 4.0 * math.log2(math.e)
CHUNK = 1024
GROUP = 16
F32 = jnp.float32
BF16 = jnp.bfloat16
VMEM = pl.BlockSpec(memory_space=pltpu.VMEM)
HBM = pl.BlockSpec(memory_space=pltpu.HBM)
SMEM = pl.BlockSpec(memory_space=pltpu.SMEM)
EW = EDGE * T
HALO = EW + EW // 2
NN = (((1,), (0,)), ((), ()))
NT = (((1,), (1,)), ((), ()))
TN = (((0,), (0,)), ((), ()))


def params(mib=48):
    return pltpu.CompilerParams(vmem_limit_bytes=mib * 1024 * 1024)


def cost(us):
    return pl.CostEstimate(flops=int(us * 1.0e9), bytes_accessed=int(us * 3.0e6), transcendentals=0)


def dot(a, b, dims=NN):
    return lax.dot_general(a, b, dims, preferred_element_type=F32)


def split2(a):
    high = a.astype(BF16)
    return high, (a - high.astype(F32)).astype(BF16)


def split3(a):
    high = a.astype(BF16).astype(F32)
    rest = a - high
    mid = rest.astype(BF16).astype(F32)
    return high, mid, rest - mid


@functools.lru_cache(maxsize=None)
def tables(length, count):
    ids = np.arange(length, dtype=np.int64)
    angle = (ids[:, None] * ids[None, :] % length).astype(np.float64) * (2.0 * np.pi / length)
    full = (np.cos(angle) + np.sin(angle)) / math.sqrt(length)
    high = full.astype(ml_dtypes.bfloat16)
    low = (full - high.astype(np.float64)).astype(ml_dtypes.bfloat16)
    block = length // count
    rows = (np.arange(count)[:, None] * block - 1 + np.arange(block + 16)[None, :]) % length
    lam = (4.0 * np.sin(np.pi * ids / length) ** 2).astype(np.float32)
    return high, low, high[rows], low[rows], lam


def places():
    r, a, count = lax.axis_index("rad"), lax.axis_index("azi"), lax.axis_size("azi")
    return r, a, lax.rem(a + count - 1, count), lax.rem(a + 1, count)


def write_edges(pos_ref, mass_ref, out_ref):
    count = out_ref.shape[0]

    def rows(part, half, width):
        lanes = pl.ds(part * EW + half * width, width)
        return jnp.concatenate([pos_ref[0:3, lanes], mass_ref[0:1, lanes]], axis=0)

    up, down = rows(1, 0, EW), rows(0, 0, EW)
    right = [rows(3, half, EW // 2) for half in range(2)]
    left = [rows(2, half, EW // 2) for half in range(2)]
    for d in range(count):
        out_ref[d, 0:4, 0:EW] = up
        out_ref[d, 4:8, 0:EW] = down
    for d in range(count):
        for half in range(2):
            out_ref[d, 4 * half : 4 * half + 4, EW : EW + EW // 2] = right[half]
    _, _, previous, _ = places()
    for half in range(2):
        out_ref[previous, 4 * half : 4 * half + 4, EW : EW + EW // 2] = left[half]


def edges_kernel(pos_ref, mass_ref, pot_ref, out_ref):
    write_edges(pos_ref, mass_ref, out_ref)
    _, _, previous, _ = places()
    turned = pot_ref[...].T
    for d in range(out_ref.shape[0]):
        out_ref[d, 0:1, HALO : HALO + G] = turned[G - 1 : G, :]
    out_ref[previous, 0:1, HALO : HALO + G] = turned[0:1, :]


def edges(pos, mass, pot, azi_count):
    return pl.pallas_call(
        edges_kernel,
        grid=(1,),
        in_specs=[
            pl.BlockSpec((3, 4 * EW), lambda i: (0, 0)),
            pl.BlockSpec((1, 4 * EW), lambda i: (0, 0)),
            pl.BlockSpec((G, G), lambda i: (0, 0)),
        ],
        out_specs=pl.BlockSpec((azi_count, 8, HALO + 128), lambda i: (0, 0, 0)),
        out_shape=jax.ShapeDtypeStruct((azi_count, 8, HALO + 128), F32),
        compiler_params=params(60),
        cost_estimate=cost(1),
        name="edges",
    )(pos, mass, pot)


def pick_kernel(s, halo, shear_ref, far_ref, *refs):
    up_ref, down_ref = refs[-2:]
    r, a, _, _ = places()
    count = far_ref.shape[0]
    up_source = lax.rem(a + count - shear_ref[s, lax.rem(r + 1, shear_ref.shape[1])], count)
    down_source = lax.rem(a + shear_ref[s, r], count)
    up_ref[:, 0:EW] = far_ref[up_source, 0:4, 0:EW]
    down_ref[:, 0:EW] = far_ref[down_source, 4:8, 0:EW]
    if halo:
        pot_ref = refs[0]
        for ref, row in ((up_ref, G - 1), (down_ref, 0)):
            ref[:, EW : EW + 128] = jnp.zeros((4, 128), F32)
            ref[0:1, EW : EW + G] = pot_ref[row : row + 1, :]


def pick(s, shear, far, *pot):
    shape = jax.ShapeDtypeStruct((4, EW + 128 * len(pot)), F32)
    return pl.pallas_call(
        functools.partial(pick_kernel, s, len(pot) > 0),
        in_specs=[SMEM] + [VMEM] * (1 + len(pot)),
        out_specs=[VMEM] * 2,
        out_shape=[shape] * 2,
        compiler_params=params(),
        cost_estimate=cost(0.5),
        name="pick",
    )(shear, far, *pot)


def density_kernel(cells_ref, mass_ref, dest_ref, dens_ref, target_ref, count_ref, acc_ref):
    lanes = cells_ref.shape[1]
    row = lax.broadcasted_iota(jnp.int32, (G, CHUNK), 0)
    acc_ref[...] = jnp.zeros_like(acc_ref)

    def body(j, carry):
        part = pl.ds(pl.multiple_of(j * CHUNK, CHUNK), CHUNK)
        mass = mass_ref[0:1, part]
        pieces = split3(mass)
        for s in range(STEPS):
            cell = cells_ref[s : s + 1, part]
            hit_x = row == (cell >> 6)
            hit_y = jnp.where(row == (cell & (G - 1)), 1.0, 0.0).astype(BF16)
            left = jnp.concatenate(
                [jnp.where(hit_x, piece, 0.0).astype(BF16) for piece in pieces], axis=0
            )
            acc_ref[s] += dot(left, hit_y, NT)
        return carry

    lax.fori_loop(0, lanes // CHUNK, body, 0, unroll=4)
    both = []
    for s in range(STEPS):
        both.append(acc_ref[s, 0:G] + acc_ref[s, G : 2 * G] + acc_ref[s, 2 * G : 3 * G])
    whole = jnp.concatenate(both, axis=1)
    dens_ref[0] = whole

    for d in range(count_ref.shape[0]):
        count_ref[d] = 0

    def slot(t, carry):
        d = dest_ref[t]
        k = count_ref[d]
        target_ref[t] = d * SLOT + k
        count_ref[d] = k + 1
        return carry

    lax.fori_loop(0, TILES, slot, 0)


def densities(cells, mass, dest, azi_count):
    return pl.pallas_call(
        density_kernel,
        in_specs=[VMEM, VMEM, SMEM],
        out_specs=[VMEM, SMEM],
        out_shape=[
            jax.ShapeDtypeStruct((1, G, 2 * G), F32),
            jax.ShapeDtypeStruct((TILES,), jnp.int32),
        ],
        scratch_shapes=[
            pltpu.SMEM((azi_count,), jnp.int32),
            pltpu.VMEM((STEPS, 3 * G, G), F32),
        ],
        compiler_params=params(),
        cost_estimate=cost(7),
        name="densities",
    )(cells, mass, dest)


def dot3(a_high, a_low, b, dims=NN):
    b_high, b_low = split2(b)
    return dot(a_high, b_high, dims) + dot(a_high, b_low, dims) + dot(a_low, b_high, dims)


def fetch(pairs, sem_ref):
    copies = [pltpu.make_async_copy(s, d, sem_ref.at[i]) for i, (s, d) in enumerate(pairs)]
    for copy in copies:
        copy.start()
    return copies


def forward_x_kernel(high_ref, low_ref, dens_ref, more_ref, out_ref, all_ref, h_ref, l_ref, sem_ref):
    r, _, _, _ = places()
    for ref, p, d in blocks_of((dens_ref, more_ref)):
        all_ref[pl.ds(pl.multiple_of(d * G, G), G)] = ref[p]
    for copy in fetch(((high_ref.at[r], h_ref), (low_ref.at[r], l_ref)), sem_ref):
        copy.wait()
    values = all_ref[...]
    lines = dot3(h_ref[1 : G + 1], l_ref[1 : G + 1], values)
    turned = lines.T
    whole = jnp.concatenate([turned[0:G], turned[G : 2 * G]], axis=1)
    for d in range(out_ref.shape[0]):
        out_ref[d] = whole


def solve_y_kernel(high_ref, low_ref, some_high_ref, some_low_ref, lam_y_ref, lam_x_ref, in_ref, out_ref,
                   h_ref, l_ref, sh_ref, sl_ref, lam_ref, modes_ref, sem_ref):
    r, a, _, _ = places()
    size = h_ref.shape[0]
    part = size // 4
    pairs = [(lam_x_ref.at[r], lam_ref)]
    for p in range(4):
        rows = pl.ds(p * part, part)
        pairs += [(high_ref.at[rows], h_ref.at[rows]), (low_ref.at[rows], l_ref.at[rows])]
    pairs += [(some_high_ref.at[a], sh_ref), (some_low_ref.at[a], sl_ref)]
    copies = fetch(pairs, sem_ref)
    values = in_ref[...].reshape(-1, 2 * G)
    copies[0].wait()
    lam_x = lam_ref[0:1, :]
    mean = jnp.sum(values, axis=0, keepdims=True) * (1.0 / size)
    values = values - jnp.where(lam_x == 0.0, mean, 0.0)
    for p in range(4):
        rows = slice(p * part, (p + 1) * part)
        copies[1 + 2 * p].wait()
        copies[2 + 2 * p].wait()
        modes = dot3(h_ref[rows], l_ref[rows], values)
        lam = lam_y_ref[rows] + lam_x
        at_zero = lam == 0.0
        modes_ref[rows] = modes * jnp.where(at_zero, 0.0, -GRAV / jnp.where(at_zero, 1.0, lam))
    copies[9].wait()
    copies[10].wait()
    lines = dot3(sh_ref[...], sl_ref[...], modes_ref[...])
    inner = lines[1 : G + 1].T
    first = jnp.concatenate([inner[0:G], inner[G : 2 * G]], axis=1)
    out_ref[0, 0:G] = first
    out_ref[0, G : G + 8] = jnp.zeros((8, 2 * G), F32)
    out_ref[0, G : G + 1] = lines[0:1]
    out_ref[0, G + 1 : G + 2] = lines[G + 1 : G + 2]


def inverse_x_kernel(high_ref, low_ref, in_ref, more_ref, grad_ref, pot_ref, all_ref, halo_ref, side_ref,
                     turn_ref, h_ref, l_ref, sem_ref):
    r, _, _, _ = places()
    copies = fetch(((high_ref.at[r], h_ref), (low_ref.at[r], l_ref)), sem_ref)
    halo_ref[...] = jnp.zeros_like(halo_ref)
    for ref, p, d in blocks_of((in_ref, more_ref)):
        all_ref[pl.ds(pl.multiple_of(d * G, G), G)] = ref[p, 0:G]
        side_ref[d] = ref[p, G : G + 8, 0:G]
    for d in range(side_ref.shape[0]):
        halo_ref[:, d * G : (d + 1) * G] = side_ref[d]
    for copy in copies:
        copy.wait()
    grid = dot3(h_ref[...], l_ref[...], all_ref[...])
    pot_ref[...] = grid[1 : G + 1, G : 2 * G]
    b_high, b_low = split2(halo_ref[...])
    a_high, a_low = h_ref[1 : G + 1], l_ref[1 : G + 1]
    sides = dot(b_high, a_high, NT) + dot(b_low, a_high, NT) + dot(b_high, a_low, NT)
    grad_x = -(grid[2 : G + 2, 0:G] - grid[0:G, 0:G]) * 0.5
    turn_ref[8 : G + 8] = grid[1 : G + 1, 0:G].T
    turn_ref[7:8] = sides[0:1]
    turn_ref[G + 8 : G + 9] = sides[1:2]
    grad_y = (-(turn_ref[9 : G + 9] - turn_ref[7 : G + 7]) * 0.5).T
    write_gradient(grad_ref, grad_x, grad_y)


def write_gradient(grad_ref, grad_x, grad_y):
    for c, part in enumerate((grad_x, grad_y)):
        for p, piece in enumerate(split3(part)):
            grad_ref[c * G : (c + 1) * G, p * G : (p + 1) * G] = piece


def solve_call(kernel, name, tables_in, arrays, outs, scratch, us):
    return pl.pallas_call(
        kernel,
        in_specs=[HBM] * len(tables_in) + [VMEM] * len(arrays),
        out_specs=[VMEM] * len(outs),
        out_shape=list(outs),
        scratch_shapes=list(scratch),
        compiler_params=params(60),
        cost_estimate=cost(us),
        name=name,
    )(*tables_in, *arrays)


def gathered(value, axis):
    count = lax.axis_size(axis)
    d = count // 2
    parts = [value]
    while d:
        whole = jnp.concatenate(parts, axis=0) if len(parts) > 1 else parts[0]
        parts = [whole, lax.ppermute(whole, axis, [(i, i ^ d) for i in range(count)])]
        d //= 2
    return parts


def blocks_of(refs):
    r, _, _, _ = places()
    half = refs[0].shape[0]
    bits = (2 * half).bit_length() - 1
    for p in range(2 * half):
        partner = sum((p >> bit & 1) << (bits - 1 - bit) for bit in range(bits))
        yield refs[p // half], p % half, r ^ partner


def exchange(value, axis):
    return lax.all_to_all(value, axis, split_axis=0, concat_axis=0, tiled=True)


def old_gradient(pot_ref, up_ref, down_ref, before, after, grad_ref, turn_ref):
    pot = pot_ref[...]
    turn_ref[8 : G + 8] = pot
    turn_ref[7:8] = up_ref[0:1, EW : EW + G]
    turn_ref[G + 8 : G + 9] = down_ref[0:1, EW : EW + G]
    grad_x = -(turn_ref[9 : G + 9] - turn_ref[7 : G + 7]) * 0.5
    turn_ref[8 : G + 8] = pot.T
    turn_ref[7:8] = before
    turn_ref[G + 8 : G + 9] = after
    grad_y = (-(turn_ref[9 : G + 9] - turn_ref[7 : G + 7]) * 0.5).T
    write_gradient(grad_ref, grad_x, grad_y)


def features(pos, mass, work_ref, i_ref, j_ref, r_ref, lanes, own):
    width = pos.shape[1]
    q = pos - 0.5
    norm = -CEXP * jnp.sum(q * q, axis=0, keepdims=True)
    one = jnp.ones_like(norm)
    n_high, n_mid, n_low = split3(norm)
    q_high, q_mid, q_low = split3(q)
    zero = jnp.zeros((8, width), F32)

    def write(groups, target_ref):
        for k, (three, last) in enumerate(groups):
            work_ref[4 * k : 4 * k + 3, 0:width] = three
            work_ref[4 * k + 3 : 4 * k + 4, 0:width] = last
        work_ref[24:32, 0:width] = zero
        target_ref[:, lanes] = work_ref[0:32, 0:width].astype(BF16)

    write(
        (
            (q_high, one),
            (q_mid, n_mid),
            (q_high, one),
            (q_low, n_low),
            (q_high, one),
            (q_mid, n_high),
        ),
        j_ref,
    )
    if own:
        a_high, a_mid, a_low = split3(q * (2.0 * CEXP))
        write(
            (
                (a_high, n_high),
                (a_high, one),
                (a_mid, n_mid),
                (a_high, one),
                (a_low, n_low),
                (a_mid, one),
            ),
            i_ref,
        )
    weighted = q * mass
    w_high = weighted.astype(BF16).astype(F32)
    m_high = mass.astype(BF16).astype(F32)
    work_ref[0:3, 0:width] = w_high
    work_ref[3:4, 0:width] = m_high
    work_ref[4:7, 0:width] = weighted - w_high
    work_ref[7:8, 0:width] = mass - m_high
    work_ref[8:16, 0:width] = zero
    r_ref[:, lanes] = work_ref[0:16, 0:width].astype(BF16)


def step_kernel(last, *refs):
    if last:
        (nbr_ref, target_ref, pos_ref, vel_ref, mass_ref, cells_ref, far_ref, up_ref, down_ref,
         grad_in_ref, pack_ref, i_ref, j_ref, r_ref, work_ref, grad_ref) = refs
    else:
        (nbr_ref, target_ref, pos_ref, vel_ref, mass_ref, cells_ref, far_ref, up_ref, down_ref,
         pot_ref, new_pos_ref, new_vel_ref, edges_ref, pack_ref,
         i_ref, j_ref, r_ref, work_ref, grad_ref, turn_ref, split_ref) = refs
    r, _, previous, following = places()
    if last:
        grad_ref[...] = grad_in_ref[...].astype(BF16)
    else:
        before = far_ref[previous, 0:1, HALO : HALO + G]
        after = far_ref[following, 0:1, HALO : HALO + G]
        old_gradient(pot_ref, up_ref, down_ref, before, after, split_ref, turn_ref)
        grad_ref[...] = split_ref[...].astype(BF16)
    pack_ref[...] = jnp.zeros_like(pack_ref)
    own_lanes = TILES * T

    def prepare(j, carry):
        lanes = pl.ds(pl.multiple_of(j * CHUNK, CHUNK), CHUNK)
        features(pos_ref[0:3, lanes], mass_ref[0:1, lanes], work_ref, i_ref, j_ref, r_ref, lanes, True)
        return carry

    lax.fori_loop(0, own_lanes // CHUNK, prepare, 0)

    first_ghost = own_lanes
    for ghost, axis, move in (
        (up_ref[0:4, 0:EW], 0, -1.0),
        (down_ref[0:4, 0:EW], 0, 1.0),
        (far_ref[previous, 0:4, EW:HALO], 1, -1.0),
        (far_ref[previous, 4:8, EW:HALO], 1, -1.0),
        (far_ref[following, 0:4, EW:HALO], 1, 1.0),
        (far_ref[following, 4:8, EW:HALO], 1, 1.0),
    ):
        width = ghost.shape[1]
        sub = lax.broadcasted_iota(jnp.int32, (3, width), 0)
        place = ghost[0:3] + jnp.where(sub == axis, move, 0.0)
        lanes = slice(first_ghost, first_ghost + width)
        features(place, ghost[3:4], work_ref, i_ref, j_ref, r_ref, lanes, False)
        first_ghost += width

    strip_x = (r - lax.axis_size("rad") // 2).astype(F32)
    row = lax.broadcasted_iota(jnp.int32, (G, T), 0)

    wide_row = lax.broadcasted_iota(jnp.int32, (G, GROUP * T), 0)

    def tiles(g, carry):
        wide = pl.ds(pl.multiple_of(g * (GROUP * T), GROUP * T), GROUP * T)
        cell = cells_ref[last : last + 1, wide]
        hit_y = jnp.where(wide_row == (cell & (G - 1)), 1.0, 0.0).astype(BF16)
        hit_x = wide_row == (cell >> 6)
        field = dot(grad_ref[...], jnp.concatenate([hit_y] * 3, axis=0))
        exponents = []
        rights = []
        for u in range(GROUP):
            t = g * GROUP + u
            own = pl.ds(pl.multiple_of(t * T, T), T)
            picks = [pl.ds(pl.multiple_of(nbr_ref[t, n] * T, T), T) for n in range(LINKS)]
            others = jnp.concatenate([j_ref[:, p] for p in picks], axis=1)
            rights.append(jnp.concatenate([r_ref[:, p] for p in picks], axis=1))
            exponents.append(dot(others, i_ref[:, own], TN))
        weights = [jnp.exp2(e).astype(BF16) for e in exponents]
        sums = jnp.concatenate([dot(x, y) for x, y in zip(rights, weights)], axis=1)
        grav_x = jnp.sum(jnp.where(hit_x, field[0:G], 0.0), axis=0, keepdims=True)
        grav_y = jnp.sum(jnp.where(hit_x, field[G : 2 * G], 0.0), axis=0, keepdims=True)
        pos = pos_ref[0:3, wide]
        vel = vel_ref[0:3, wide]
        total = sums[0:4] + sums[4:8]
        contact = STIFF * ((pos - 0.5) * total[3:4] - total[0:3])
        acc_x = contact[0:1] + grav_x + 2.0 * OMEGA * vel[1:2] + 3.0 * OMEGA**2 * (pos[0:1] + strip_x)
        acc_y = contact[1:2] + grav_y - 2.0 * OMEGA * vel[0:1]
        acc_z = contact[2:3] - OMEGA**2 * (pos[2:3] - 0.5)
        speed = vel + DT * jnp.concatenate([acc_x, acc_y, acc_z], axis=0)
        if not last:
            place = pos + DT * speed
            new_pos_ref[0:3, wide] = place
            new_vel_ref[0:3, wide] = speed
        for u in range(GROUP):
            target = target_ref[g * GROUP + u]
            d = target // SLOT
            k = target % SLOT
            part = slice(u * T, (u + 1) * T)
            if last:
                for c in range(3):
                    pack_ref[d, pl.ds(k * 3 + c, 1), :] = speed[c : c + 1, part]
            else:
                pack_ref[d, k, 0:3, :] = place[:, part]
                pack_ref[d, k, 3:4, :] = mass_ref[0:1, pl.ds(pl.multiple_of(g * (GROUP * T) + u * T, T), T)]
        return carry

    lax.fori_loop(0, TILES // GROUP, tiles, 0)
    if not last:
        write_edges(new_pos_ref, mass_ref, edges_ref)


def step(last, nbr, target, pos, vel, mass, cells, far, up, down, more, azi_count):
    lanes = TILES * T
    if last:
        outs = [jax.ShapeDtypeStruct((azi_count, SLOT * 3, T), F32)]
        out_specs = [VMEM]
    else:
        outs = [jax.ShapeDtypeStruct((3, lanes), F32)] * 2
        outs += [jax.ShapeDtypeStruct((azi_count, 8, HALO), F32)]
        outs += [jax.ShapeDtypeStruct((azi_count, SLOT, 4, T), F32)]
        out_specs = [VMEM] * 4
    scratch = [
        pltpu.VMEM((32, lanes), BF16),
        pltpu.VMEM((32, lanes + GHOSTS * T), BF16),
        pltpu.VMEM((16, lanes + GHOSTS * T), BF16),
        pltpu.VMEM((32, CHUNK), F32),
        pltpu.VMEM((2 * G, 3 * G), BF16),
    ]
    if not last:
        scratch += [pltpu.VMEM((G + 16, G), F32), pltpu.VMEM((2 * G, 3 * G), F32)]
    return pl.pallas_call(
        functools.partial(step_kernel, last),
        in_specs=[SMEM] * 2 + [VMEM] * (7 + len(more)),
        out_specs=out_specs,
        out_shape=outs,
        scratch_shapes=scratch,
        compiler_params=params(),
        cost_estimate=cost(14),
        name=f"step_{last}",
    )(nbr, target, pos, vel, mass, cells, far, up, down, *more)


def assemble_kernel(azi_count, place_ref, speed_ref, out_ref):
    _, b, _, _ = places()

    def group(g, carry):
        a = g // (SLOT // 8)
        h = g % (SLOT // 8)
        signed = lax.rem(a - b + azi_count // 2 + azi_count, azi_count) - azi_count // 2
        move = signed.astype(F32)
        speeds = speed_ref[a, pl.ds(pl.multiple_of(h * 24, 8), 24), :]
        sub = lax.broadcasted_iota(jnp.int32, (3, T), 0)
        for k in range(8):
            four = place_ref[a, h * 8 + k]
            speed = speeds[3 * k : 3 * k + 3]
            mass = four[3:4]
            place = four[0:3] + DT * speed
            place = place + jnp.where((sub == 1) & (mass > 0.0), move, 0.0)
            lanes = pl.ds(pl.multiple_of((g * 8 + k) * T, T), T)
            out_ref[0:3, lanes] = place
            out_ref[3:6, lanes] = speed
            out_ref[6:7, lanes] = mass
        return carry

    lax.fori_loop(0, azi_count * SLOT // 8, group, 0)


def assemble(place, speed):
    azi_count = place.shape[0]
    return pl.pallas_call(
        functools.partial(assemble_kernel, azi_count),
        in_specs=[VMEM, VMEM],
        out_specs=VMEM,
        out_shape=jax.ShapeDtypeStruct((7, azi_count * SLOT * T), F32),
        compiler_params=params(),
        cost_estimate=cost(4),
        name="assemble",
    )(place, speed)


def shifted(value, axis, steps):
    count = lax.axis_size(axis)
    return lax.ppermute(value, axis, [(i, (i + steps) % count) for i in range(count)])


def local(positions, velocities, masses, neighbours, shear_offsets, destinations, deposit_cells, old_potential):
    rad_count = lax.axis_size("rad")
    azi_count = lax.axis_size("azi")
    mass = masses.reshape(1, -1)

    sent = edges(positions, mass, old_potential, azi_count)
    cells_after, sent = lax.optimization_barrier((deposit_cells, sent))
    far = exchange(sent, "azi")
    dens, target = densities(cells_after, mass, destinations, azi_count)
    up, down = pick(0, shear_offsets, far, old_potential)
    up, down = shifted(up, "rad", 1), shifted(down, "rad", -1)

    high_x, low_x, rows_high_x, rows_low_x, lam_x = tables(G * rad_count, rad_count)
    high_y, low_y, rows_high_y, rows_low_y, lam_y = tables(G * azi_count, azi_count)
    lam_cols = np.tile(lam_x.reshape(rad_count, 1, G), (1, 8, 2))
    lam_rows = np.ascontiguousarray(np.broadcast_to(lam_y[:, None], (G * azi_count, 2 * G)))
    size_x, size_y = G * rad_count, G * azi_count
    block = lambda size: pltpu.VMEM((G + 16, size), BF16)
    dens, dens_more = gathered(dens, "rad")
    dens, dens_more, far = lax.optimization_barrier((dens, dens_more, far))
    (lines,) = solve_call(
        forward_x_kernel, "forward_x", (rows_high_x, rows_low_x), (dens, dens_more),
        (jax.ShapeDtypeStruct((azi_count, G, 2 * G), F32),),
        (pltpu.VMEM((size_x, 2 * G), F32), block(size_x), block(size_x), pltpu.SemaphoreType.DMA((2,))), 2,
    )
    lines = exchange(lines, "azi")
    place, speed, sent_1, pack_place = step(
        0, neighbours, target, positions, velocities, mass, deposit_cells, far, up, down,
        (old_potential,), azi_count,
    )
    lines, sent_1 = lax.optimization_barrier((lines, sent_1))
    far_1 = exchange(sent_1, "azi")
    full = pltpu.VMEM((size_y, size_y), BF16)
    (solved,) = pl.pallas_call(
        solve_y_kernel,
        in_specs=[HBM] * 4 + [VMEM, HBM, VMEM],
        out_specs=[VMEM],
        out_shape=[jax.ShapeDtypeStruct((1, G + 8, 2 * G), F32)],
        scratch_shapes=[
            full, full, block(size_y), block(size_y), pltpu.VMEM((8, 2 * G), F32),
            pltpu.VMEM((size_y, 2 * G), F32), pltpu.SemaphoreType.DMA((11,)),
        ],
        compiler_params=params(60),
        cost_estimate=cost(5),
        name="solve_y",
    )(high_y, low_y, rows_high_y, rows_low_y, lam_rows, lam_cols, lines)
    solved, solved_more = gathered(solved, "rad")
    gradient, potential = solve_call(
        inverse_x_kernel, "inverse_x", (rows_high_x, rows_low_x), (solved, solved_more),
        (jax.ShapeDtypeStruct((2 * G, 3 * G), F32), jax.ShapeDtypeStruct((G, G), F32)),
        (pltpu.VMEM((size_x, 2 * G), F32), pltpu.VMEM((8, size_x), F32),
         pltpu.VMEM((rad_count, 8, G), F32), pltpu.VMEM((G + 16, G), F32),
         block(size_x), block(size_x), pltpu.SemaphoreType.DMA((2,))), 2,
    )

    up_1, down_1 = pick(1, shear_offsets, far_1)
    pack_place, up_1, down_1 = lax.optimization_barrier((pack_place, up_1, down_1))
    up_1, down_1 = shifted(up_1, "rad", 1), shifted(down_1, "rad", -1)
    pack_place = exchange(pack_place, "azi")
    (pack_speed,) = step(
        1, neighbours, target, place, speed, mass, deposit_cells, far_1, up_1, down_1,
        (gradient,), azi_count,
    )
    pack_place, pack_speed = lax.optimization_barrier((pack_place, pack_speed))
    pack_speed = exchange(pack_speed, "azi")
    return assemble(pack_place, pack_speed), potential


def solution(mesh):
    placed = (
        P(None, ("rad", "azi")),
        P(None, ("rad", "azi")),
        P(("rad", "azi")),
        P(("rad", "azi"), None),
        P(),
        P(("rad", "azi")),
        P(None, ("rad", "azi")),
        P("rad", "azi"),
    )
    return jax.shard_map(
        local,
        mesh=mesh,
        in_specs=placed,
        out_specs=(P(None, ("rad", "azi")), P("rad", "azi")),
        check_vma=False,
    )
```

```python
import functools
import math

import jax
import jax.numpy as jnp
import ml_dtypes
import numpy as np
from jax import lax
from jax.experimental import pallas as pl
from jax.experimental.pallas import tpu as pltpu
from jax.sharding import PartitionSpec as P

T = 128
TILES = 128
EDGE = 4
LINKS = 4
GHOSTS = 16
G = 64
SLOT = 32
STEPS = 2
DT = 0.1
OMEGA = 0.3
STIFF = 0.15
GRAV = 0.01
CEXP = 4.0 * math.log2(math.e)
CHUNK = 1024
GROUP = 16
F32 = jnp.float32
BF16 = jnp.bfloat16
VMEM = pl.BlockSpec(memory_space=pltpu.VMEM)
HBM = pl.BlockSpec(memory_space=pltpu.HBM)
SMEM = pl.BlockSpec(memory_space=pltpu.SMEM)
EW = EDGE * T
HALO = EW + EW // 2
NN = (((1,), (0,)), ((), ()))
NT = (((1,), (1,)), ((), ()))
TN = (((0,), (0,)), ((), ()))


def params(mib=48):
    return pltpu.CompilerParams(vmem_limit_bytes=mib * 1024 * 1024)


def cost(us):
    return pl.CostEstimate(flops=int(us * 1.0e9), bytes_accessed=int(us * 3.0e6), transcendentals=0)


def dot(a, b, dims=NN):
    return lax.dot_general(a, b, dims, preferred_element_type=F32)


def split2(a):
    high = a.astype(BF16)
    return high, (a - high.astype(F32)).astype(BF16)


def split3(a):
    high = a.astype(BF16).astype(F32)
    rest = a - high
    mid = rest.astype(BF16).astype(F32)
    return high, mid, rest - mid


@functools.lru_cache(maxsize=None)
def tables(length, count):
    ids = np.arange(length, dtype=np.int64)
    angle = (ids[:, None] * ids[None, :] % length).astype(np.float64) * (2.0 * np.pi / length)
    full = (np.cos(angle) + np.sin(angle)) / math.sqrt(length)
    high = full.astype(ml_dtypes.bfloat16)
    low = (full - high.astype(np.float64)).astype(ml_dtypes.bfloat16)
    block = length // count
    rows = (np.arange(count)[:, None] * block - 1 + np.arange(block + 16)[None, :]) % length
    return high[rows], low[rows]


@functools.lru_cache(maxsize=None)
def powers(length, count, far_length, far_count):
    block = length // count
    lam = 4.0 * np.sin(np.pi * np.arange(length) / length) ** 2
    half = 0.5 * lam
    q = 1.0 / (1.0 + half + np.sqrt(half * (half + 2.0)))
    q[0] = 0.0
    q = np.tile(q.reshape(count, 1, block), (1, 1, STEPS))
    y = np.arange(G)[None, :, None]
    strips = np.arange(far_count)[None, :, None]
    safe = np.where(q == 0.0, 0.5, q)
    rows = [
        q ** (y + 1),
        np.where(q == 0.0, 0.0, q ** (G * strips) / (1.0 - q**far_length)),
        q,
        np.where(q == 0.0, 0.0, -GRAV / (1.0 / safe - safe)),
        q ** (2 ** np.arange(6)[None, :, None]),
        q ** (G - y),
    ]
    return np.concatenate(rows, axis=1).astype(np.float32)


def places():
    r, a, count = lax.axis_index("rad"), lax.axis_index("azi"), lax.axis_size("azi")
    return r, a, lax.rem(a + count - 1, count), lax.rem(a + 1, count)


def write_edges(pos_ref, mass_ref, out_ref):
    count = out_ref.shape[0]

    def rows(part, half, width):
        lanes = pl.ds(part * EW + half * width, width)
        return jnp.concatenate([pos_ref[0:3, lanes], mass_ref[0:1, lanes]], axis=0)

    up, down = rows(1, 0, EW), rows(0, 0, EW)
    right = [rows(3, half, EW // 2) for half in range(2)]
    left = [rows(2, half, EW // 2) for half in range(2)]
    for d in range(count):
        out_ref[d, 0:4, 0:EW] = up
        out_ref[d, 4:8, 0:EW] = down
    for d in range(count):
        for half in range(2):
            out_ref[d, 4 * half : 4 * half + 4, EW : EW + EW // 2] = right[half]
    _, _, previous, _ = places()
    for half in range(2):
        out_ref[previous, 4 * half : 4 * half + 4, EW : EW + EW // 2] = left[half]


def edges_kernel(pos_ref, mass_ref, pot_ref, out_ref):
    write_edges(pos_ref, mass_ref, out_ref)
    _, _, previous, _ = places()
    turned = pot_ref[...].T
    for d in range(out_ref.shape[0]):
        out_ref[d, 0:1, HALO : HALO + G] = turned[G - 1 : G, :]
    out_ref[previous, 0:1, HALO : HALO + G] = turned[0:1, :]


def edges(pos, mass, pot, azi_count):
    return pl.pallas_call(
        edges_kernel,
        grid=(1,),
        in_specs=[
            pl.BlockSpec((3, 4 * EW), lambda i: (0, 0)),
            pl.BlockSpec((1, 4 * EW), lambda i: (0, 0)),
            pl.BlockSpec((G, G), lambda i: (0, 0)),
        ],
        out_specs=pl.BlockSpec((azi_count, 8, HALO + 128), lambda i: (0, 0, 0)),
        out_shape=jax.ShapeDtypeStruct((azi_count, 8, HALO + 128), F32),
        compiler_params=params(60),
        cost_estimate=cost(1),
        name="edges",
    )(pos, mass, pot)


def pick_kernel(s, halo, shear_ref, far_ref, *refs):
    up_ref, down_ref = refs[-2:]
    r, a, _, _ = places()
    count = far_ref.shape[0]
    up_source = lax.rem(a + count - shear_ref[s, lax.rem(r + 1, shear_ref.shape[1])], count)
    down_source = lax.rem(a + shear_ref[s, r], count)
    up_ref[:, 0:EW] = far_ref[up_source, 0:4, 0:EW]
    down_ref[:, 0:EW] = far_ref[down_source, 4:8, 0:EW]
    if halo:
        pot_ref = refs[0]
        for ref, row in ((up_ref, G - 1), (down_ref, 0)):
            ref[:, EW : EW + 128] = jnp.zeros((4, 128), F32)
            ref[0:1, EW : EW + G] = pot_ref[row : row + 1, :]


def pick(s, shear, far, *pot):
    shape = jax.ShapeDtypeStruct((4, EW + 128 * len(pot)), F32)
    return pl.pallas_call(
        functools.partial(pick_kernel, s, len(pot) > 0),
        in_specs=[SMEM] + [VMEM] * (1 + len(pot)),
        out_specs=[VMEM] * 2,
        out_shape=[shape] * 2,
        compiler_params=params(),
        cost_estimate=cost(0.5),
        name="pick",
    )(shear, far, *pot)


def density_kernel(cells_ref, mass_ref, dest_ref, dens_ref, target_ref, count_ref, acc_ref):
    lanes = cells_ref.shape[1]
    row = lax.broadcasted_iota(jnp.int32, (G, CHUNK), 0)
    acc_ref[...] = jnp.zeros_like(acc_ref)

    def body(j, carry):
        part = pl.ds(pl.multiple_of(j * CHUNK, CHUNK), CHUNK)
        mass = mass_ref[0:1, part]
        pieces = split3(mass)
        for s in range(STEPS):
            cell = cells_ref[s : s + 1, part]
            hit_x = row == (cell >> 6)
            hit_y = jnp.where(row == (cell & (G - 1)), 1.0, 0.0).astype(BF16)
            left = jnp.concatenate(
                [jnp.where(hit_x, piece, 0.0).astype(BF16) for piece in pieces], axis=0
            )
            acc_ref[s] += dot(left, hit_y, NT)
        return carry

    lax.fori_loop(0, lanes // CHUNK, body, 0, unroll=4)
    both = []
    for s in range(STEPS):
        both.append(acc_ref[s, 0:G] + acc_ref[s, G : 2 * G] + acc_ref[s, 2 * G : 3 * G])
    whole = jnp.concatenate(both, axis=1)
    dens_ref[0] = whole

    for d in range(count_ref.shape[0]):
        count_ref[d] = 0

    def slot(t, carry):
        d = dest_ref[t]
        k = count_ref[d]
        target_ref[t] = d * SLOT + k
        count_ref[d] = k + 1
        return carry

    lax.fori_loop(0, TILES, slot, 0)


def densities(cells, mass, dest, azi_count):
    return pl.pallas_call(
        density_kernel,
        in_specs=[VMEM, VMEM, SMEM],
        out_specs=[VMEM, SMEM],
        out_shape=[
            jax.ShapeDtypeStruct((1, G, 2 * G), F32),
            jax.ShapeDtypeStruct((TILES,), jnp.int32),
        ],
        scratch_shapes=[
            pltpu.SMEM((azi_count,), jnp.int32),
            pltpu.VMEM((STEPS, 3 * G, G), F32),
        ],
        compiler_params=params(),
        cost_estimate=cost(0.3),
        name="densities",
    )(cells, mass, dest)


def dot3(a_high, a_low, b, dims=NN):
    b_high, b_low = split2(b)
    return dot(a_high, b_high, dims) + dot(a_high, b_low, dims) + dot(a_low, b_high, dims)


def fetch(pairs, sem_ref):
    copies = [pltpu.make_async_copy(s, d, sem_ref.at[i]) for i, (s, d) in enumerate(pairs)]
    for copy in copies:
        copy.start()
    return copies


def forward_x_kernel(high_ref, low_ref, power_ref, dens_ref, more_ref, edges_ref, sums_ref, sent_ref,
                     ends_ref, all_ref, scan_ref, h_ref, l_ref, p_ref, sem_ref):
    r, _, _, _ = places()
    copies = fetch(((high_ref.at[r], h_ref), (low_ref.at[r], l_ref), (power_ref.at[r], p_ref)), sem_ref)
    for ref, p, d in blocks_of((dens_ref, more_ref)):
        all_ref[pl.ds(pl.multiple_of(d * G, G), G)] = ref[p]
    for copy in copies:
        copy.wait()
    lines = dot3(h_ref[1 : G + 1], l_ref[1 : G + 1], all_ref[...])
    turned = lines.T
    value = jnp.concatenate([turned[0:G], turned[G : 2 * G]], axis=1)
    doubling = p_ref.shape[0] - G - 6
    scan_ref[...] = jnp.zeros_like(scan_ref)
    for way in range(2):
        total = value
        for j in range(6):
            scan_ref[32 : 32 + G] = total
            first = 32 + (1 << j) * (1 if way else -1)
            total = total + p_ref[doubling + j : doubling + j + 1] * scan_ref[first : first + G]
        sums_ref[way] = total
    sums_ref[2] = value
    ends_ref[0:1] = sums_ref[0, G - 1 : G]
    ends_ref[1:2] = sums_ref[1, 0:1]
    ends_ref[2:3] = lines[0:1]
    ends_ref[3:8] = jnp.zeros((5, 2 * G), F32)
    for d in range(sent_ref.shape[0]):
        sent_ref[d, :, 0:HALO] = edges_ref[d]
        sent_ref[d, :, HALO : HALO + 2 * G] = ends_ref[...]


def solve_y_kernel(power_ref, far_ref, sums_ref, out_ref, p_ref, line_ref, sem_ref):
    r, a, _, _ = places()
    copies = fetch(((power_ref.at[r], p_ref),), sem_ref)
    count = far_ref.shape[0]
    size = count * G
    lanes = slice(HALO, HALO + 2 * G)
    row = lax.broadcasted_iota(jnp.int32, (G + 8, G), 0)
    lane = lax.broadcasted_iota(jnp.int32, (G + 8, G), 1)
    constant = []
    for s in range(STEPS):
        parts = [far_ref[b, 2:3, HALO + s * G : HALO + (s + 1) * G] for b in range(count)]
        mean = jnp.sum(sum(parts), axis=1, keepdims=True) * (1.0 / size)
        total = jnp.zeros((G + 8, G), F32)
        for b in range(count):
            n = (a - b) * G + row - 1 - lane
            n = jnp.where(n < 0, n + size, n)
            total += (n * (size - n)).astype(F32) * (parts[b] - mean)
        constant.append(jnp.sum(total, axis=1, keepdims=True) * (GRAV / (2.0 * size)))
    copies[0].wait()
    start = jnp.zeros((1, 2 * G), F32)
    stop = jnp.zeros((1, 2 * G), F32)
    for m in range(count):
        weight = p_ref[G + m : G + m + 1]
        start += weight * far_ref[lax.rem(a + 2 * count - 1 - m, count), 0:1, lanes]
        stop += weight * far_ref[lax.rem(a + 1 + m, count), 1:2, lanes]
    q = p_ref[G + count : G + count + 1]
    scale = p_ref[G + count + 1 : G + count + 2]
    rising = sums_ref[0] + p_ref[0:G] * start
    falling = sums_ref[1] + p_ref[p_ref.shape[0] - G : p_ref.shape[0]] * stop
    line_ref[...] = jnp.zeros_like(line_ref)
    line_ref[0:1] = (start + q * falling[0:1]) * scale
    line_ref[1 : G + 1] = (rising + falling - sums_ref[2]) * scale
    line_ref[G + 1 : G + 2] = (stop + q * rising[G - 1 : G]) * scale
    lines = line_ref[...]
    mode = lax.broadcasted_iota(jnp.int32, lines.shape, 1) + jnp.where(r == 0, 0, 4 * G)
    for s in range(STEPS):
        lines = jnp.where(mode == s * G, constant[s], lines)
    inner = lines[1 : G + 1].T
    out_ref[0, 0:G] = jnp.concatenate([inner[0:G], inner[G : 2 * G]], axis=1)
    out_ref[0, G : G + 8] = jnp.zeros((8, 2 * G), F32)
    out_ref[0, G : G + 1] = lines[0:1]
    out_ref[0, G + 1 : G + 2] = lines[G + 1 : G + 2]


def inverse_x_kernel(high_ref, low_ref, in_ref, more_ref, grad_ref, pot_ref, all_ref, halo_ref, side_ref,
                     turn_ref, h_ref, l_ref, sem_ref):
    r, _, _, _ = places()
    copies = fetch(((high_ref.at[r], h_ref), (low_ref.at[r], l_ref)), sem_ref)
    halo_ref[...] = jnp.zeros_like(halo_ref)
    for ref, p, d in blocks_of((in_ref, more_ref)):
        all_ref[pl.ds(pl.multiple_of(d * G, G), G)] = ref[p, 0:G]
        side_ref[d] = ref[p, G : G + 8, 0:G]
    for d in range(side_ref.shape[0]):
        halo_ref[:, d * G : (d + 1) * G] = side_ref[d]
    for copy in copies:
        copy.wait()
    grid = dot3(h_ref[...], l_ref[...], all_ref[...])
    pot_ref[...] = grid[1 : G + 1, G : 2 * G]
    b_high, b_low = split2(halo_ref[...])
    a_high, a_low = h_ref[1 : G + 1], l_ref[1 : G + 1]
    sides = dot(b_high, a_high, NT) + dot(b_low, a_high, NT) + dot(b_high, a_low, NT)
    grad_x = -(grid[2 : G + 2, 0:G] - grid[0:G, 0:G]) * 0.5
    turn_ref[8 : G + 8] = grid[1 : G + 1, 0:G].T
    turn_ref[7:8] = sides[0:1]
    turn_ref[G + 8 : G + 9] = sides[1:2]
    grad_y = (-(turn_ref[9 : G + 9] - turn_ref[7 : G + 7]) * 0.5).T
    write_gradient(grad_ref, grad_x, grad_y)


def write_gradient(grad_ref, grad_x, grad_y):
    for c, part in enumerate((grad_x, grad_y)):
        for p, piece in enumerate(split3(part)):
            grad_ref[c * G : (c + 1) * G, p * G : (p + 1) * G] = piece


def solve_call(kernel, name, tables_in, arrays, outs, scratch, us):
    return pl.pallas_call(
        kernel,
        in_specs=[HBM] * len(tables_in) + [VMEM] * len(arrays),
        out_specs=[VMEM] * len(outs),
        out_shape=list(outs),
        scratch_shapes=list(scratch),
        compiler_params=params(60),
        cost_estimate=cost(us),
        name=name,
    )(*tables_in, *arrays)


def gathered(value, axis, after=None, stage=0):
    count = lax.axis_size(axis)
    d = count // 2
    parts = [value]
    while d:
        whole = jnp.concatenate(parts, axis=0) if len(parts) > 1 else parts[0]
        if after is not None and d == count >> stage:
            whole, after = lax.optimization_barrier((whole, after))
        parts = [whole, lax.ppermute(whole, axis, [(i, i ^ d) for i in range(count)])]
        d //= 2
    return *parts, after


def blocks_of(refs):
    r, _, _, _ = places()
    half = refs[0].shape[0]
    bits = (2 * half).bit_length() - 1
    for p in range(2 * half):
        partner = sum((p >> bit & 1) << (bits - 1 - bit) for bit in range(bits))
        yield refs[p // half], p % half, r ^ partner


def exchange(value, axis):
    return lax.all_to_all(value, axis, split_axis=0, concat_axis=0, tiled=True)


def old_gradient(pot_ref, up_ref, down_ref, before, after, grad_ref, turn_ref):
    pot = pot_ref[...]
    turn_ref[8 : G + 8] = pot
    turn_ref[7:8] = up_ref[0:1, EW : EW + G]
    turn_ref[G + 8 : G + 9] = down_ref[0:1, EW : EW + G]
    grad_x = -(turn_ref[9 : G + 9] - turn_ref[7 : G + 7]) * 0.5
    turn_ref[8 : G + 8] = pot.T
    turn_ref[7:8] = before
    turn_ref[G + 8 : G + 9] = after
    grad_y = (-(turn_ref[9 : G + 9] - turn_ref[7 : G + 7]) * 0.5).T
    write_gradient(grad_ref, grad_x, grad_y)


def features(pos, mass, work_ref, i_ref, j_ref, r_ref, lanes, own):
    width = pos.shape[1]
    q = pos - 0.5
    norm = -CEXP * jnp.sum(q * q, axis=0, keepdims=True)
    one = jnp.ones_like(norm)
    n_high, n_mid, n_low = split3(norm)
    q_high, q_mid, q_low = split3(q)
    zero = jnp.zeros((8, width), F32)

    def write(groups, target_ref):
        for k, (three, last) in enumerate(groups):
            work_ref[4 * k : 4 * k + 3, 0:width] = three
            work_ref[4 * k + 3 : 4 * k + 4, 0:width] = last
        work_ref[24:32, 0:width] = zero
        target_ref[:, lanes] = work_ref[0:32, 0:width].astype(BF16)

    write(
        (
            (q_high, one),
            (q_mid, n_mid),
            (q_high, one),
            (q_low, n_low),
            (q_high, one),
            (q_mid, n_high),
        ),
        j_ref,
    )
    if own:
        a_high, a_mid, a_low = split3(q * (2.0 * CEXP))
        write(
            (
                (a_high, n_high),
                (a_high, one),
                (a_mid, n_mid),
                (a_high, one),
                (a_low, n_low),
                (a_mid, one),
            ),
            i_ref,
        )
    weighted = q * mass
    w_high = weighted.astype(BF16).astype(F32)
    m_high = mass.astype(BF16).astype(F32)
    work_ref[0:3, 0:width] = w_high
    work_ref[3:4, 0:width] = m_high
    work_ref[4:7, 0:width] = weighted - w_high
    work_ref[7:8, 0:width] = mass - m_high
    work_ref[8:16, 0:width] = zero
    r_ref[:, lanes] = work_ref[0:16, 0:width].astype(BF16)


def step_kernel(last, *refs):
    if last:
        (nbr_ref, target_ref, pos_ref, vel_ref, mass_ref, cells_ref, far_ref, up_ref, down_ref,
         grad_in_ref, pack_ref, i_ref, j_ref, r_ref, work_ref, grad_ref) = refs
    else:
        (nbr_ref, target_ref, pos_ref, vel_ref, mass_ref, cells_ref, far_ref, up_ref, down_ref,
         pot_ref, new_pos_ref, new_vel_ref, edges_ref, pack_ref,
         i_ref, j_ref, r_ref, work_ref, grad_ref, turn_ref, split_ref) = refs
    r, _, previous, following = places()
    if last:
        grad_ref[...] = grad_in_ref[...].astype(BF16)
    else:
        before = far_ref[previous, 0:1, HALO : HALO + G]
        after = far_ref[following, 0:1, HALO : HALO + G]
        old_gradient(pot_ref, up_ref, down_ref, before, after, split_ref, turn_ref)
        grad_ref[...] = split_ref[...].astype(BF16)
    pack_ref[...] = jnp.zeros_like(pack_ref)
    own_lanes = TILES * T

    def prepare(j, carry):
        lanes = pl.ds(pl.multiple_of(j * CHUNK, CHUNK), CHUNK)
        features(pos_ref[0:3, lanes], mass_ref[0:1, lanes], work_ref, i_ref, j_ref, r_ref, lanes, True)
        return carry

    lax.fori_loop(0, own_lanes // CHUNK, prepare, 0)

    first_ghost = own_lanes
    for ghost, axis, move in (
        (up_ref[0:4, 0:EW], 0, -1.0),
        (down_ref[0:4, 0:EW], 0, 1.0),
        (far_ref[previous, 0:4, EW:HALO], 1, -1.0),
        (far_ref[previous, 4:8, EW:HALO], 1, -1.0),
        (far_ref[following, 0:4, EW:HALO], 1, 1.0),
        (far_ref[following, 4:8, EW:HALO], 1, 1.0),
    ):
        width = ghost.shape[1]
        sub = lax.broadcasted_iota(jnp.int32, (3, width), 0)
        place = ghost[0:3] + jnp.where(sub == axis, move, 0.0)
        lanes = slice(first_ghost, first_ghost + width)
        features(place, ghost[3:4], work_ref, i_ref, j_ref, r_ref, lanes, False)
        first_ghost += width

    strip_x = (r - lax.axis_size("rad") // 2).astype(F32)
    row = lax.broadcasted_iota(jnp.int32, (G, T), 0)

    wide_row = lax.broadcasted_iota(jnp.int32, (G, GROUP * T), 0)

    def tiles(g, carry):
        wide = pl.ds(pl.multiple_of(g * (GROUP * T), GROUP * T), GROUP * T)
        cell = cells_ref[last : last + 1, wide]
        hit_y = jnp.where(wide_row == (cell & (G - 1)), 1.0, 0.0).astype(BF16)
        hit_x = wide_row == (cell >> 6)
        field = dot(grad_ref[...], jnp.concatenate([hit_y] * 3, axis=0))
        exponents = []
        rights = []
        for u in range(GROUP):
            t = g * GROUP + u
            own = pl.ds(pl.multiple_of(t * T, T), T)
            picks = [pl.ds(pl.multiple_of(nbr_ref[t, n] * T, T), T) for n in range(LINKS)]
            others = jnp.concatenate([j_ref[:, p] for p in picks], axis=1)
            rights.append(jnp.concatenate([r_ref[:, p] for p in picks], axis=1))
            exponents.append(dot(others, i_ref[:, own], TN))
        weights = [jnp.exp2(e).astype(BF16) for e in exponents]
        sums = jnp.concatenate([dot(x, y) for x, y in zip(rights, weights)], axis=1)
        grav_x = jnp.sum(jnp.where(hit_x, field[0:G], 0.0), axis=0, keepdims=True)
        grav_y = jnp.sum(jnp.where(hit_x, field[G : 2 * G], 0.0), axis=0, keepdims=True)
        pos = pos_ref[0:3, wide]
        vel = vel_ref[0:3, wide]
        total = sums[0:4] + sums[4:8]
        contact = STIFF * ((pos - 0.5) * total[3:4] - total[0:3])
        acc_x = contact[0:1] + grav_x + 2.0 * OMEGA * vel[1:2] + 3.0 * OMEGA**2 * (pos[0:1] + strip_x)
        acc_y = contact[1:2] + grav_y - 2.0 * OMEGA * vel[0:1]
        acc_z = contact[2:3] - OMEGA**2 * (pos[2:3] - 0.5)
        speed = vel + DT * jnp.concatenate([acc_x, acc_y, acc_z], axis=0)
        if not last:
            place = pos + DT * speed
            new_pos_ref[0:3, wide] = place
            new_vel_ref[0:3, wide] = speed
        for u in range(GROUP):
            target = target_ref[g * GROUP + u]
            d = target // SLOT
            k = target % SLOT
            part = slice(u * T, (u + 1) * T)
            if last:
                for c in range(3):
                    pack_ref[d, pl.ds(k * 3 + c, 1), :] = speed[c : c + 1, part]
            else:
                pack_ref[d, k, 0:3, :] = place[:, part]
                pack_ref[d, k, 3:4, :] = mass_ref[0:1, pl.ds(pl.multiple_of(g * (GROUP * T) + u * T, T), T)]
        return carry

    lax.fori_loop(0, TILES // GROUP, tiles, 0)
    if not last:
        write_edges(new_pos_ref, mass_ref, edges_ref)


def step(last, nbr, target, pos, vel, mass, cells, far, up, down, more, azi_count):
    lanes = TILES * T
    if last:
        outs = [jax.ShapeDtypeStruct((azi_count, SLOT * 3, T), F32)]
        out_specs = [VMEM]
    else:
        outs = [jax.ShapeDtypeStruct((3, lanes), F32)] * 2
        outs += [jax.ShapeDtypeStruct((azi_count, 8, HALO), F32)]
        outs += [jax.ShapeDtypeStruct((azi_count, SLOT, 4, T), F32)]
        out_specs = [VMEM] * 4
    scratch = [
        pltpu.VMEM((32, lanes), BF16),
        pltpu.VMEM((32, lanes + GHOSTS * T), BF16),
        pltpu.VMEM((16, lanes + GHOSTS * T), BF16),
        pltpu.VMEM((32, CHUNK), F32),
        pltpu.VMEM((2 * G, 3 * G), BF16),
    ]
    if not last:
        scratch += [pltpu.VMEM((G + 16, G), F32), pltpu.VMEM((2 * G, 3 * G), F32)]
    return pl.pallas_call(
        functools.partial(step_kernel, last),
        in_specs=[SMEM] * 2 + [VMEM] * (7 + len(more)),
        out_specs=out_specs,
        out_shape=outs,
        scratch_shapes=scratch,
        compiler_params=params(),
        cost_estimate=cost(14),
        name=f"step_{last}",
    )(nbr, target, pos, vel, mass, cells, far, up, down, *more)


def assemble_kernel(azi_count, place_ref, speed_ref, out_ref):
    _, b, _, _ = places()

    def group(g, carry):
        a = g // (SLOT // 8)
        h = g % (SLOT // 8)
        signed = lax.rem(a - b + azi_count // 2 + azi_count, azi_count) - azi_count // 2
        move = signed.astype(F32)
        speeds = speed_ref[a, pl.ds(pl.multiple_of(h * 24, 8), 24), :]
        sub = lax.broadcasted_iota(jnp.int32, (3, T), 0)
        for k in range(8):
            four = place_ref[a, h * 8 + k]
            speed = speeds[3 * k : 3 * k + 3]
            mass = four[3:4]
            place = four[0:3] + DT * speed
            place = place + jnp.where((sub == 1) & (mass > 0.0), move, 0.0)
            lanes = pl.ds(pl.multiple_of((g * 8 + k) * T, T), T)
            out_ref[0:3, lanes] = place
            out_ref[3:6, lanes] = speed
            out_ref[6:7, lanes] = mass
        return carry

    lax.fori_loop(0, azi_count * SLOT // 8, group, 0)


def assemble(place, speed):
    azi_count = place.shape[0]
    return pl.pallas_call(
        functools.partial(assemble_kernel, azi_count),
        in_specs=[VMEM, VMEM],
        out_specs=VMEM,
        out_shape=jax.ShapeDtypeStruct((7, azi_count * SLOT * T), F32),
        compiler_params=params(),
        cost_estimate=cost(4),
        name="assemble",
    )(place, speed)


def shifted(value, axis, steps):
    count = lax.axis_size(axis)
    return lax.ppermute(value, axis, [(i, (i + steps) % count) for i in range(count)])


def local(positions, velocities, masses, neighbours, shear_offsets, destinations, deposit_cells, old_potential):
    rad_count = lax.axis_size("rad")
    azi_count = lax.axis_size("azi")
    mass = masses.reshape(1, -1)

    sent = edges(positions, mass, old_potential, azi_count)
    cells_after, sent = lax.optimization_barrier((deposit_cells, sent))
    far = exchange(sent, "azi")
    dens, target = densities(cells_after, mass, destinations, azi_count)

    rows_high, rows_low = tables(G * rad_count, rad_count)
    power = powers(G * rad_count, rad_count, G * azi_count, azi_count)
    size_x = G * rad_count
    block = pltpu.VMEM((G + 16, size_x), BF16)
    power_block = pltpu.VMEM(power.shape[1:], F32)
    up, down = pick(0, shear_offsets, far, old_potential)
    dens, dens_more, (up, down) = gathered(dens, "rad", (up, down), 3)
    up, down = shifted(up, "rad", 1), shifted(down, "rad", -1)
    place, speed, edges_1, pack_place = step(
        0, neighbours, target, positions, velocities, mass, deposit_cells, far, up, down, (old_potential,), azi_count,
    )
    sums, sent_1 = solve_call(
        forward_x_kernel, "forward_x", (rows_high, rows_low, power), (dens, dens_more, edges_1),
        (jax.ShapeDtypeStruct((3, G, 2 * G), F32), jax.ShapeDtypeStruct((azi_count, 8, HALO + 2 * G), F32)),
        (pltpu.VMEM((8, 2 * G), F32), pltpu.VMEM((size_x, 2 * G), F32), pltpu.VMEM((2 * G, 2 * G), F32), block, block,
         power_block, pltpu.SemaphoreType.DMA((3,))), 2,
    )
    far_1 = exchange(sent_1, "azi")
    up_1, down_1 = pick(1, shear_offsets, far_1)
    (solved,) = solve_call(
        solve_y_kernel, "solve_y", (power,), (far_1, sums),
        (jax.ShapeDtypeStruct((1, G + 8, 2 * G), F32),),
        (power_block, pltpu.VMEM((G + 8, 2 * G), F32), pltpu.SemaphoreType.DMA((1,))), 2,
    )
    solved, solved_more, _ = gathered(solved, "rad")
    gradient, potential = solve_call(
        inverse_x_kernel, "inverse_x", (rows_high, rows_low), (solved, solved_more),
        (jax.ShapeDtypeStruct((2 * G, 3 * G), F32), jax.ShapeDtypeStruct((G, G), F32)),
        (pltpu.VMEM((size_x, 2 * G), F32), pltpu.VMEM((8, size_x), F32),
         pltpu.VMEM((rad_count, 8, G), F32), pltpu.VMEM((G + 16, G), F32),
         block, block, pltpu.SemaphoreType.DMA((2,))), 2,
    )

    pack_place, up_1, down_1 = lax.optimization_barrier((pack_place, up_1, down_1))
    up_1, down_1 = shifted(up_1, "rad", 1), shifted(down_1, "rad", -1)
    pack_place = exchange(pack_place, "azi")
    (pack_speed,) = step(
        1, neighbours, target, place, speed, mass, deposit_cells, far_1, up_1, down_1,
        (gradient,), azi_count,
    )
    pack_place, pack_speed = lax.optimization_barrier((pack_place, pack_speed))
    pack_speed = exchange(pack_speed, "azi")
    return assemble(pack_place, pack_speed), potential


def solution(mesh):
    placed = (
        P(None, ("rad", "azi")),
        P(None, ("rad", "azi")),
        P(("rad", "azi")),
        P(("rad", "azi"), None),
        P(),
        P(("rad", "azi")),
        P(None, ("rad", "azi")),
        P("rad", "azi"),
    )
    return jax.shard_map(
        local,
        mesh=mesh,
        in_specs=placed,
        out_specs=(P(None, ("rad", "azi")), P("rad", "azi")),
        check_vma=False,
    )
```

```python
import functools
import math

import jax
import jax.numpy as jnp
import ml_dtypes
import numpy as np
from jax import lax
from jax.experimental import pallas as pl
from jax.experimental.pallas import tpu as pltpu
from jax.sharding import PartitionSpec as P

T = 128
TILES = 128
EDGE = 4
LINKS = 4
GHOSTS = 16
G = 64
SLOT = 32
STEPS = 2
DT = 0.1
OMEGA = 0.3
STIFF = 0.15
GRAV = 0.01
CEXP = 4.0 * math.log2(math.e)
CHUNK = 1024
GROUP = 16
F32 = jnp.float32
BF16 = jnp.bfloat16
VMEM = pl.BlockSpec(memory_space=pltpu.VMEM)
HBM = pl.BlockSpec(memory_space=pltpu.HBM)
SMEM = pl.BlockSpec(memory_space=pltpu.SMEM)
EW = EDGE * T
HALO = EW + EW // 2
NN = (((1,), (0,)), ((), ()))
NT = (((1,), (1,)), ((), ()))
TN = (((0,), (0,)), ((), ()))


def params(mib=48):
    return pltpu.CompilerParams(vmem_limit_bytes=mib * 1024 * 1024)


def cost(us):
    return pl.CostEstimate(flops=int(us * 1.0e9), bytes_accessed=int(us * 3.0e6), transcendentals=0)


def dot(a, b, dims=NN):
    return lax.dot_general(a, b, dims, preferred_element_type=F32)


def split2(a):
    high = a.astype(BF16)
    return high, (a - high.astype(F32)).astype(BF16)


def split3(a):
    high = a.astype(BF16).astype(F32)
    rest = a - high
    mid = rest.astype(BF16).astype(F32)
    return high, mid, rest - mid


@functools.lru_cache(maxsize=None)
def tables(length, count):
    ids = np.arange(length, dtype=np.int64)
    angle = (ids[:, None] * ids[None, :] % length).astype(np.float64) * (2.0 * np.pi / length)
    full = (np.cos(angle) + np.sin(angle)) / math.sqrt(length)
    high = full.astype(ml_dtypes.bfloat16)
    low = (full - high.astype(np.float64)).astype(ml_dtypes.bfloat16)
    block = length // count
    rows = (np.arange(count)[:, None] * block - 1 + np.arange(block + 16)[None, :]) % length
    return high[rows], low[rows]


@functools.lru_cache(maxsize=None)
def powers(length, count, far_length, far_count):
    block = length // count
    lam = 4.0 * np.sin(np.pi * np.arange(length) / length) ** 2
    half = 0.5 * lam
    q = 1.0 / (1.0 + half + np.sqrt(half * (half + 2.0)))
    q[0] = 0.0
    q = np.tile(q.reshape(count, 1, block), (1, 1, STEPS))
    y = np.arange(G)[None, :, None]
    strips = np.arange(far_count)[None, :, None]
    safe = np.where(q == 0.0, 0.5, q)
    rows = [
        q ** (y + 1),
        np.where(q == 0.0, 0.0, q ** (G * strips) / (1.0 - q**far_length)),
        q,
        np.where(q == 0.0, 0.0, -GRAV / (1.0 / safe - safe)),
        q ** (2 ** np.arange(6)[None, :, None]),
        q ** (G - y),
    ]
    return np.concatenate(rows, axis=1).astype(np.float32)


def places():
    r, a, count = lax.axis_index("rad"), lax.axis_index("azi"), lax.axis_size("azi")
    return r, a, lax.rem(a + count - 1, count), lax.rem(a + 1, count)


def write_edges(pos_ref, mass_ref, out_ref):
    count = out_ref.shape[0]

    def rows(part, half, width):
        lanes = pl.ds(part * EW + half * width, width)
        return jnp.concatenate([pos_ref[0:3, lanes], mass_ref[0:1, lanes]], axis=0)

    up, down = rows(1, 0, EW), rows(0, 0, EW)
    right = [rows(3, half, EW // 2) for half in range(2)]
    left = [rows(2, half, EW // 2) for half in range(2)]
    for d in range(count):
        out_ref[d, 0:4, 0:EW] = up
        out_ref[d, 4:8, 0:EW] = down
    for d in range(count):
        for half in range(2):
            out_ref[d, 4 * half : 4 * half + 4, EW : EW + EW // 2] = right[half]
    _, _, previous, _ = places()
    for half in range(2):
        out_ref[previous, 4 * half : 4 * half + 4, EW : EW + EW // 2] = left[half]


def edges_kernel(pos_ref, mass_ref, pot_ref, out_ref):
    write_edges(pos_ref, mass_ref, out_ref)
    _, _, previous, _ = places()
    turned = pot_ref[...].T
    for d in range(out_ref.shape[0]):
        out_ref[d, 0:1, HALO : HALO + G] = turned[G - 1 : G, :]
    out_ref[previous, 0:1, HALO : HALO + G] = turned[0:1, :]


def edges(pos, mass, pot, azi_count):
    return pl.pallas_call(
        edges_kernel,
        grid=(1,),
        in_specs=[
            pl.BlockSpec((3, 4 * EW), lambda i: (0, 0)),
            pl.BlockSpec((1, 4 * EW), lambda i: (0, 0)),
            pl.BlockSpec((G, G), lambda i: (0, 0)),
        ],
        out_specs=pl.BlockSpec((azi_count, 8, HALO + 128), lambda i: (0, 0, 0)),
        out_shape=jax.ShapeDtypeStruct((azi_count, 8, HALO + 128), F32),
        compiler_params=params(60),
        cost_estimate=cost(1),
        name="edges",
    )(pos, mass, pot)


def pick_kernel(s, halo, shear_ref, far_ref, *refs):
    up_ref, down_ref = refs[-2:]
    r, a, _, _ = places()
    count = far_ref.shape[0]
    up_source = lax.rem(a + count - shear_ref[s, lax.rem(r + 1, shear_ref.shape[1])], count)
    down_source = lax.rem(a + shear_ref[s, r], count)
    up_ref[:, 0:EW] = far_ref[up_source, 0:4, 0:EW]
    down_ref[:, 0:EW] = far_ref[down_source, 4:8, 0:EW]
    if halo:
        pot_ref = refs[0]
        for ref, row in ((up_ref, G - 1), (down_ref, 0)):
            ref[:, EW : EW + 128] = jnp.zeros((4, 128), F32)
            ref[0:1, EW : EW + G] = pot_ref[row : row + 1, :]


def pick(s, shear, far, *pot):
    shape = jax.ShapeDtypeStruct((4, EW + 128 * len(pot)), F32)
    return pl.pallas_call(
        functools.partial(pick_kernel, s, len(pot) > 0),
        in_specs=[SMEM] + [VMEM] * (1 + len(pot)),
        out_specs=[VMEM] * 2,
        out_shape=[shape] * 2,
        compiler_params=params(),
        cost_estimate=cost(0.5),
        name="pick",
    )(shear, far, *pot)


def density_kernel(cells_ref, mass_ref, dest_ref, dens_ref, target_ref, count_ref, acc_ref):
    lanes = cells_ref.shape[1]
    row = lax.broadcasted_iota(jnp.int32, (G, CHUNK), 0)
    acc_ref[...] = jnp.zeros_like(acc_ref)

    def body(j, carry):
        part = pl.ds(pl.multiple_of(j * CHUNK, CHUNK), CHUNK)
        mass = mass_ref[0:1, part]
        pieces = split3(mass)
        for s in range(STEPS):
            cell = cells_ref[s : s + 1, part]
            hit_x = row == (cell >> 6)
            hit_y = jnp.where(row == (cell & (G - 1)), 1.0, 0.0).astype(BF16)
            left = jnp.concatenate(
                [jnp.where(hit_x, piece, 0.0).astype(BF16) for piece in pieces], axis=0
            )
            acc_ref[s] += dot(left, hit_y, NT)
        return carry

    lax.fori_loop(0, lanes // CHUNK, body, 0, unroll=4)
    both = []
    for s in range(STEPS):
        both.append(acc_ref[s, 0:G] + acc_ref[s, G : 2 * G] + acc_ref[s, 2 * G : 3 * G])
    whole = jnp.concatenate(both, axis=1)
    dens_ref[0] = whole

    for d in range(count_ref.shape[0]):
        count_ref[d] = 0

    def slot(t, carry):
        d = dest_ref[t]
        k = count_ref[d]
        target_ref[t] = d * SLOT + k
        count_ref[d] = k + 1
        return carry

    lax.fori_loop(0, TILES, slot, 0)


def densities(cells, mass, dest, azi_count):
    return pl.pallas_call(
        density_kernel,
        in_specs=[VMEM, VMEM, SMEM],
        out_specs=[VMEM, SMEM],
        out_shape=[
            jax.ShapeDtypeStruct((1, G, 2 * G), F32),
            jax.ShapeDtypeStruct((TILES,), jnp.int32),
        ],
        scratch_shapes=[
            pltpu.SMEM((azi_count,), jnp.int32),
            pltpu.VMEM((STEPS, 3 * G, G), F32),
        ],
        compiler_params=params(),
        cost_estimate=cost(0.3),
        name="densities",
    )(cells, mass, dest)


def dot3(a_high, a_low, b, dims=NN):
    b_high, b_low = split2(b)
    return dot(a_high, b_high, dims) + dot(a_high, b_low, dims) + dot(a_low, b_high, dims)


def fetch(pairs, sem_ref):
    copies = [pltpu.make_async_copy(s, d, sem_ref.at[i]) for i, (s, d) in enumerate(pairs)]
    for copy in copies:
        copy.start()
    return copies


def forward_x_kernel(high_ref, low_ref, power_ref, dens_ref, more_ref, edges_ref, sums_ref, sent_ref,
                     ends_ref, all_ref, scan_ref, h_ref, l_ref, p_ref, sem_ref):
    r, _, _, _ = places()
    pairs = [(high_ref.at[r], h_ref), (low_ref.at[r], l_ref), (power_ref.at[r], p_ref)]
    for ref, p, d in blocks_of((dens_ref, more_ref)):
        pairs.append((ref.at[p], all_ref.at[pl.ds(pl.multiple_of(d * G, G), G)]))
    copies = fetch(pairs, sem_ref)
    for copy in copies:
        copy.wait()
    lines = dot3(h_ref[1 : G + 1], l_ref[1 : G + 1], all_ref[...])
    turned = lines.T
    value = jnp.concatenate([turned[0:G], turned[G : 2 * G]], axis=1)
    doubling = p_ref.shape[0] - G - 6
    scan_ref[...] = jnp.zeros_like(scan_ref)
    for way in range(2):
        total = value
        for j in range(6):
            scan_ref[32 : 32 + G] = total
            first = 32 + (1 << j) * (1 if way else -1)
            total = total + p_ref[doubling + j : doubling + j + 1] * scan_ref[first : first + G]
        sums_ref[way] = total
    sums_ref[2] = value
    ends_ref[0:1] = sums_ref[0, G - 1 : G]
    ends_ref[1:2] = sums_ref[1, 0:1]
    ends_ref[2:3] = lines[0:1]
    ends_ref[3:8] = jnp.zeros((5, 2 * G), F32)
    for d in range(sent_ref.shape[0]):
        sent_ref[d, :, 0:HALO] = edges_ref[d]
        sent_ref[d, :, HALO : HALO + 2 * G] = ends_ref[...]


def solve_y_kernel(power_ref, far_ref, sums_ref, out_ref, p_ref, line_ref, sem_ref):
    r, a, _, _ = places()
    copies = fetch(((power_ref.at[r], p_ref),), sem_ref)
    count = far_ref.shape[0]
    size = count * G
    lanes = slice(HALO, HALO + 2 * G)
    row = lax.broadcasted_iota(jnp.int32, (G + 8, G), 0)
    lane = lax.broadcasted_iota(jnp.int32, (G + 8, G), 1)
    constant = []
    for s in range(STEPS):
        parts = [far_ref[b, 2:3, HALO + s * G : HALO + (s + 1) * G] for b in range(count)]
        mean = jnp.sum(sum(parts), axis=1, keepdims=True) * (1.0 / size)
        total = jnp.zeros((G + 8, G), F32)
        for b in range(count):
            n = (a - b) * G + row - 1 - lane
            n = jnp.where(n < 0, n + size, n)
            total += ((n * (size - n)).astype(F32) - (size * size - 1) / 6.0) * (parts[b] - mean)
        constant.append(jnp.sum(total, axis=1, keepdims=True) * (GRAV / (2.0 * size)))
    copies[0].wait()
    start = jnp.zeros((1, 2 * G), F32)
    stop = jnp.zeros((1, 2 * G), F32)
    for m in range(count):
        weight = p_ref[G + m : G + m + 1]
        start += weight * far_ref[lax.rem(a + 2 * count - 1 - m, count), 0:1, lanes]
        stop += weight * far_ref[lax.rem(a + 1 + m, count), 1:2, lanes]
    q = p_ref[G + count : G + count + 1]
    scale = p_ref[G + count + 1 : G + count + 2]
    rising = sums_ref[0] + p_ref[0:G] * start
    falling = sums_ref[1] + p_ref[p_ref.shape[0] - G : p_ref.shape[0]] * stop
    line_ref[...] = jnp.zeros_like(line_ref)
    line_ref[0:1] = (start + q * falling[0:1]) * scale
    line_ref[1 : G + 1] = (rising + falling - sums_ref[2]) * scale
    line_ref[G + 1 : G + 2] = (stop + q * rising[G - 1 : G]) * scale
    lines = line_ref[...]
    mode = lax.broadcasted_iota(jnp.int32, lines.shape, 1) + jnp.where(r == 0, 0, 4 * G)
    for s in range(STEPS):
        lines = jnp.where(mode == s * G, constant[s], lines)
    inner = lines[1 : G + 1].T
    out_ref[0, 0:G] = jnp.concatenate([inner[0:G], inner[G : 2 * G]], axis=1)
    out_ref[0, G : G + 8] = jnp.zeros((8, 2 * G), F32)
    out_ref[0, G : G + 1] = lines[0:1]
    out_ref[0, G + 1 : G + 2] = lines[G + 1 : G + 2]


def inverse_x_kernel(high_ref, low_ref, in_ref, more_ref, grad_ref, pot_ref, all_ref, halo_ref, blocks_ref,
                     turn_ref, h_ref, l_ref, sem_ref):
    r, _, _, _ = places()
    pairs = [(high_ref.at[r], h_ref), (low_ref.at[r], l_ref)]
    for ref, p, d in blocks_of((in_ref, more_ref)):
        pairs.append((ref.at[p], blocks_ref.at[d]))
    copies = fetch(pairs, sem_ref)
    halo_ref[...] = jnp.zeros_like(halo_ref)
    for copy in copies:
        copy.wait()
    for d in range(blocks_ref.shape[0]):
        all_ref[d * G : (d + 1) * G] = blocks_ref[d, 0:G]
        halo_ref[:, d * G : (d + 1) * G] = blocks_ref[d, G : G + 8, 0:G]
    grid = dot3(h_ref[...], l_ref[...], all_ref[...])
    pot_ref[...] = grid[1 : G + 1, G : 2 * G]
    b_high, b_low = split2(halo_ref[...])
    a_high, a_low = h_ref[1 : G + 1], l_ref[1 : G + 1]
    sides = dot(b_high, a_high, NT) + dot(b_low, a_high, NT) + dot(b_high, a_low, NT)
    grad_x = -(grid[2 : G + 2, 0:G] - grid[0:G, 0:G]) * 0.5
    turn_ref[8 : G + 8] = grid[1 : G + 1, 0:G].T
    turn_ref[7:8] = sides[0:1]
    turn_ref[G + 8 : G + 9] = sides[1:2]
    grad_y = (-(turn_ref[9 : G + 9] - turn_ref[7 : G + 7]) * 0.5).T
    write_gradient(grad_ref, grad_x, grad_y)


def write_gradient(grad_ref, grad_x, grad_y):
    for c, part in enumerate((grad_x, grad_y)):
        for p, piece in enumerate(split3(part)):
            grad_ref[c * G : (c + 1) * G, p * G : (p + 1) * G] = piece


def solve_call(kernel, name, tables_in, arrays, outs, scratch, us):
    return pl.pallas_call(
        kernel,
        in_specs=[HBM] * len(tables_in) + [VMEM] * len(arrays),
        out_specs=[VMEM] * len(outs),
        out_shape=list(outs),
        scratch_shapes=list(scratch),
        compiler_params=params(60),
        cost_estimate=cost(us),
        name=name,
    )(*tables_in, *arrays)


def gathered(value, axis, after=None, stage=0):
    count = lax.axis_size(axis)
    d = count // 2
    parts = [value]
    while d:
        whole = jnp.concatenate(parts, axis=0) if len(parts) > 1 else parts[0]
        if after is not None and d == count >> stage:
            whole, after = lax.optimization_barrier((whole, after))
        parts = [whole, lax.ppermute(whole, axis, [(i, i ^ d) for i in range(count)])]
        d //= 2
    return *parts, after


def blocks_of(refs):
    r, _, _, _ = places()
    half = refs[0].shape[0]
    bits = (2 * half).bit_length() - 1
    for p in range(2 * half):
        partner = sum((p >> bit & 1) << (bits - 1 - bit) for bit in range(bits))
        yield refs[p // half], p % half, r ^ partner


def exchange(value, axis):
    return lax.all_to_all(value, axis, split_axis=0, concat_axis=0, tiled=True)


def old_gradient(pot_ref, up_ref, down_ref, before, after, grad_ref, turn_ref):
    pot = pot_ref[...]
    turn_ref[8 : G + 8] = pot
    turn_ref[7:8] = up_ref[0:1, EW : EW + G]
    turn_ref[G + 8 : G + 9] = down_ref[0:1, EW : EW + G]
    grad_x = -(turn_ref[9 : G + 9] - turn_ref[7 : G + 7]) * 0.5
    turn_ref[8 : G + 8] = pot.T
    turn_ref[7:8] = before
    turn_ref[G + 8 : G + 9] = after
    grad_y = (-(turn_ref[9 : G + 9] - turn_ref[7 : G + 7]) * 0.5).T
    write_gradient(grad_ref, grad_x, grad_y)


def features(pos, mass, work_ref, i_ref, j_ref, r_ref, lanes, own):
    width = pos.shape[1]
    q = pos - 0.5
    norm = -CEXP * jnp.sum(q * q, axis=0, keepdims=True)
    one = jnp.ones_like(norm)
    n_high, n_mid, n_low = split3(norm)
    q_high, q_mid, q_low = split3(q)
    zero = jnp.zeros((8, width), F32)

    def write(groups, target_ref):
        for k, (three, last) in enumerate(groups):
            work_ref[4 * k : 4 * k + 3, 0:width] = three
            work_ref[4 * k + 3 : 4 * k + 4, 0:width] = last
        work_ref[24:32, 0:width] = zero
        target_ref[:, lanes] = work_ref[0:32, 0:width].astype(BF16)

    write(
        (
            (q_high, one),
            (q_mid, n_mid),
            (q_high, one),
            (q_low, n_low),
            (q_high, one),
            (q_mid, n_high),
        ),
        j_ref,
    )
    if own:
        a_high, a_mid, a_low = split3(q * (2.0 * CEXP))
        write(
            (
                (a_high, n_high),
                (a_high, one),
                (a_mid, n_mid),
                (a_high, one),
                (a_low, n_low),
                (a_mid, one),
            ),
            i_ref,
        )
    weighted = q * mass
    w_high = weighted.astype(BF16).astype(F32)
    m_high = mass.astype(BF16).astype(F32)
    work_ref[0:3, 0:width] = w_high
    work_ref[3:4, 0:width] = m_high
    work_ref[4:7, 0:width] = weighted - w_high
    work_ref[7:8, 0:width] = mass - m_high
    work_ref[8:16, 0:width] = zero
    r_ref[:, lanes] = work_ref[0:16, 0:width].astype(BF16)


def step_kernel(last, *refs):
    if last:
        (nbr_ref, target_ref, pos_ref, vel_ref, mass_ref, cells_ref, far_ref, up_ref, down_ref,
         grad_in_ref, pack_ref, i_ref, j_ref, r_ref, work_ref, grad_ref) = refs
    else:
        (nbr_ref, target_ref, pos_ref, vel_ref, mass_ref, cells_ref, far_ref, up_ref, down_ref,
         pot_ref, new_pos_ref, new_vel_ref, edges_ref, pack_ref,
         i_ref, j_ref, r_ref, work_ref, grad_ref, turn_ref, split_ref) = refs
    r, _, previous, following = places()
    if last:
        grad_ref[...] = grad_in_ref[...].astype(BF16)
    else:
        before = far_ref[previous, 0:1, HALO : HALO + G]
        after = far_ref[following, 0:1, HALO : HALO + G]
        old_gradient(pot_ref, up_ref, down_ref, before, after, split_ref, turn_ref)
        grad_ref[...] = split_ref[...].astype(BF16)
    pack_ref[...] = jnp.zeros_like(pack_ref)
    own_lanes = TILES * T

    def prepare(j, carry):
        lanes = pl.ds(pl.multiple_of(j * CHUNK, CHUNK), CHUNK)
        features(pos_ref[0:3, lanes], mass_ref[0:1, lanes], work_ref, i_ref, j_ref, r_ref, lanes, True)
        return carry

    lax.fori_loop(0, own_lanes // CHUNK, prepare, 0)

    first_ghost = own_lanes
    for ghost, axis, move in (
        (up_ref[0:4, 0:EW], 0, -1.0),
        (down_ref[0:4, 0:EW], 0, 1.0),
        (far_ref[previous, 0:4, EW:HALO], 1, -1.0),
        (far_ref[previous, 4:8, EW:HALO], 1, -1.0),
        (far_ref[following, 0:4, EW:HALO], 1, 1.0),
        (far_ref[following, 4:8, EW:HALO], 1, 1.0),
    ):
        width = ghost.shape[1]
        sub = lax.broadcasted_iota(jnp.int32, (3, width), 0)
        place = ghost[0:3] + jnp.where(sub == axis, move, 0.0)
        lanes = slice(first_ghost, first_ghost + width)
        features(place, ghost[3:4], work_ref, i_ref, j_ref, r_ref, lanes, False)
        first_ghost += width

    strip_x = (r - lax.axis_size("rad") // 2).astype(F32)
    row = lax.broadcasted_iota(jnp.int32, (G, T), 0)

    wide_row = lax.broadcasted_iota(jnp.int32, (G, GROUP * T), 0)

    def tiles(g, carry):
        wide = pl.ds(pl.multiple_of(g * (GROUP * T), GROUP * T), GROUP * T)
        cell = cells_ref[last : last + 1, wide]
        hit_y = jnp.where(wide_row == (cell & (G - 1)), 1.0, 0.0).astype(BF16)
        hit_x = wide_row == (cell >> 6)
        field = dot(grad_ref[...], jnp.concatenate([hit_y] * 3, axis=0))
        exponents = []
        rights = []
        for u in range(GROUP):
            t = g * GROUP + u
            own = pl.ds(pl.multiple_of(t * T, T), T)
            picks = [pl.ds(pl.multiple_of(nbr_ref[t, n] * T, T), T) for n in range(LINKS)]
            others = jnp.concatenate([j_ref[:, p] for p in picks], axis=1)
            rights.append(jnp.concatenate([r_ref[:, p] for p in picks], axis=1))
            exponents.append(dot(others, i_ref[:, own], TN))
        weights = [jnp.exp2(e).astype(BF16) for e in exponents]
        sums = jnp.concatenate([dot(x, y) for x, y in zip(rights, weights)], axis=1)
        grav_x = jnp.sum(jnp.where(hit_x, field[0:G], 0.0), axis=0, keepdims=True)
        grav_y = jnp.sum(jnp.where(hit_x, field[G : 2 * G], 0.0), axis=0, keepdims=True)
        pos = pos_ref[0:3, wide]
        vel = vel_ref[0:3, wide]
        total = sums[0:4] + sums[4:8]
        contact = STIFF * ((pos - 0.5) * total[3:4] - total[0:3])
        acc_x = contact[0:1] + grav_x + 2.0 * OMEGA * vel[1:2] + 3.0 * OMEGA**2 * (pos[0:1] + strip_x)
        acc_y = contact[1:2] + grav_y - 2.0 * OMEGA * vel[0:1]
        acc_z = contact[2:3] - OMEGA**2 * (pos[2:3] - 0.5)
        speed = vel + DT * jnp.concatenate([acc_x, acc_y, acc_z], axis=0)
        if not last:
            place = pos + DT * speed
            new_pos_ref[0:3, wide] = place
            new_vel_ref[0:3, wide] = speed
        for u in range(GROUP):
            target = target_ref[g * GROUP + u]
            d = target // SLOT
            k = target % SLOT
            part = slice(u * T, (u + 1) * T)
            if last:
                for c in range(3):
                    pack_ref[d, pl.ds(k * 3 + c, 1), :] = speed[c : c + 1, part]
            else:
                pack_ref[d, k, 0:3, :] = place[:, part]
                pack_ref[d, k, 3:4, :] = mass_ref[0:1, pl.ds(pl.multiple_of(g * (GROUP * T) + u * T, T), T)]
        return carry

    lax.fori_loop(0, TILES // GROUP, tiles, 0)
    if not last:
        write_edges(new_pos_ref, mass_ref, edges_ref)


def step(last, nbr, target, pos, vel, mass, cells, far, up, down, more, azi_count):
    lanes = TILES * T
    if last:
        outs = [jax.ShapeDtypeStruct((azi_count, SLOT * 3, T), F32)]
        out_specs = [VMEM]
    else:
        outs = [jax.ShapeDtypeStruct((3, lanes), F32)] * 2
        outs += [jax.ShapeDtypeStruct((azi_count, 8, HALO), F32)]
        outs += [jax.ShapeDtypeStruct((azi_count, SLOT, 4, T), F32)]
        out_specs = [VMEM] * 4
    scratch = [
        pltpu.VMEM((32, lanes), BF16),
        pltpu.VMEM((32, lanes + GHOSTS * T), BF16),
        pltpu.VMEM((16, lanes + GHOSTS * T), BF16),
        pltpu.VMEM((32, CHUNK), F32),
        pltpu.VMEM((2 * G, 3 * G), BF16),
    ]
    if not last:
        scratch += [pltpu.VMEM((G + 16, G), F32), pltpu.VMEM((2 * G, 3 * G), F32)]
    return pl.pallas_call(
        functools.partial(step_kernel, last),
        in_specs=[SMEM] * 2 + [VMEM] * (7 + len(more)),
        out_specs=out_specs,
        out_shape=outs,
        scratch_shapes=scratch,
        compiler_params=params(),
        cost_estimate=cost(14),
        name=f"step_{last}",
    )(nbr, target, pos, vel, mass, cells, far, up, down, *more)


def assemble_kernel(azi_count, place_ref, speed_ref, out_ref):
    _, b, _, _ = places()

    def group(g, carry):
        a = g // (SLOT // 8)
        h = g % (SLOT // 8)
        signed = lax.rem(a - b + azi_count // 2 + azi_count, azi_count) - azi_count // 2
        move = signed.astype(F32)
        speeds = speed_ref[a, pl.ds(pl.multiple_of(h * 24, 8), 24), :]
        sub = lax.broadcasted_iota(jnp.int32, (3, T), 0)
        for k in range(8):
            four = place_ref[a, h * 8 + k]
            speed = speeds[3 * k : 3 * k + 3]
            mass = four[3:4]
            place = four[0:3] + DT * speed
            place = place + jnp.where((sub == 1) & (mass > 0.0), move, 0.0)
            lanes = pl.ds(pl.multiple_of((g * 8 + k) * T, T), T)
            out_ref[0:3, lanes] = place
            out_ref[3:6, lanes] = speed
            out_ref[6:7, lanes] = mass
        return carry

    lax.fori_loop(0, azi_count * SLOT // 8, group, 0)


def assemble(place, speed):
    azi_count = place.shape[0]
    return pl.pallas_call(
        functools.partial(assemble_kernel, azi_count),
        in_specs=[VMEM, VMEM],
        out_specs=VMEM,
        out_shape=jax.ShapeDtypeStruct((7, azi_count * SLOT * T), F32),
        compiler_params=params(),
        cost_estimate=cost(4),
        name="assemble",
    )(place, speed)


def shifted(value, axis, steps):
    count = lax.axis_size(axis)
    return lax.ppermute(value, axis, [(i, (i + steps) % count) for i in range(count)])


def local(positions, velocities, masses, neighbours, shear_offsets, destinations, deposit_cells, old_potential):
    rad_count = lax.axis_size("rad")
    azi_count = lax.axis_size("azi")
    mass = masses.reshape(1, -1)

    sent = edges(positions, mass, old_potential, azi_count)
    cells_after, sent = lax.optimization_barrier((deposit_cells, sent))
    far = exchange(sent, "azi")
    dens, target = densities(cells_after, mass, destinations, azi_count)

    rows_high, rows_low = tables(G * rad_count, rad_count)
    power = powers(G * rad_count, rad_count, G * azi_count, azi_count)
    size_x = G * rad_count
    block = pltpu.VMEM((G + 16, size_x), BF16)
    power_block = pltpu.VMEM(power.shape[1:], F32)
    up, down = pick(0, shear_offsets, far, old_potential)
    dens, dens_more, (up, down) = gathered(dens, "rad", (up, down), 3)
    up, down = shifted(up, "rad", 1), shifted(down, "rad", -1)
    place, speed, edges_1, pack_place = step(
        0, neighbours, target, positions, velocities, mass, deposit_cells, far, up, down, (old_potential,), azi_count,
    )
    sums, sent_1 = solve_call(
        forward_x_kernel, "forward_x", (rows_high, rows_low, power, dens, dens_more), (edges_1,),
        (jax.ShapeDtypeStruct((3, G, 2 * G), F32), jax.ShapeDtypeStruct((azi_count, 8, HALO + 2 * G), F32)),
        (pltpu.VMEM((8, 2 * G), F32), pltpu.VMEM((size_x, 2 * G), F32), pltpu.VMEM((2 * G, 2 * G), F32), block, block,
         power_block, pltpu.SemaphoreType.DMA((3 + rad_count,))), 2,
    )
    far_1 = exchange(sent_1, "azi")
    up_1, down_1 = pick(1, shear_offsets, far_1)
    (solved,) = solve_call(
        solve_y_kernel, "solve_y", (power,), (far_1, sums),
        (jax.ShapeDtypeStruct((1, G + 8, 2 * G), F32),),
        (power_block, pltpu.VMEM((G + 8, 2 * G), F32), pltpu.SemaphoreType.DMA((1,))), 2,
    )
    solved, solved_more, (up_1, down_1) = gathered(solved, "rad", (up_1, down_1), 1)
    gradient, potential = solve_call(
        inverse_x_kernel, "inverse_x", (rows_high, rows_low, solved, solved_more), (),
        (jax.ShapeDtypeStruct((2 * G, 3 * G), F32), jax.ShapeDtypeStruct((G, G), F32)),
        (pltpu.VMEM((size_x, 2 * G), F32), pltpu.VMEM((8, size_x), F32),
         pltpu.VMEM((rad_count, G + 8, 2 * G), F32), pltpu.VMEM((G + 16, G), F32),
         block, block, pltpu.SemaphoreType.DMA((2 + rad_count,))), 2,
    )

    pack_place, up_1, down_1 = lax.optimization_barrier((pack_place, up_1, down_1))
    up_1, down_1 = shifted(up_1, "rad", 1), shifted(down_1, "rad", -1)
    pack_place = exchange(pack_place, "azi")
    (pack_speed,) = step(
        1, neighbours, target, place, speed, mass, deposit_cells, far_1, up_1, down_1,
        (gradient,), azi_count,
    )
    pack_place, pack_speed = lax.optimization_barrier((pack_place, pack_speed))
    pack_speed = exchange(pack_speed, "azi")
    return assemble(pack_place, pack_speed), potential


def solution(mesh):
    placed = (
        P(None, ("rad", "azi")),
        P(None, ("rad", "azi")),
        P(("rad", "azi")),
        P(("rad", "azi"), None),
        P(),
        P(("rad", "azi")),
        P(None, ("rad", "azi")),
        P("rad", "azi"),
    )
    return jax.shard_map(
        local,
        mesh=mesh,
        in_specs=placed,
        out_specs=(P(None, ("rad", "azi")), P("rad", "azi")),
        check_vma=False,
    )
```
